32 devices in a mesh: seq: 16 (over z, x, core), head: 2 (over y).
Axes of the slice: x: 2, y: 2, z: 4, core: 2. Of those that a mesh axis runs over, the one named last changes fastest.
Arguments:
- queries: bfloat16 [4096, 1024], P(('seq', 'head')), may hold values from -10 to 10, as said below
- keys: bfloat16 [4096, 1024], P(('seq', 'head')), may hold values from -8 to 8, as said below
- values: bfloat16 [4096, 1024], P(('seq', 'head')), may hold values from -6 to 6
- grad_out: bfloat16 [4096, 1024], P(('seq', 'head')), may hold values from -6 to 6
- doc_ids: int32 [4096], replicated, may hold values from 0 to 2, never falling along the last dimension, each value on 1 to 2048 neighbouring positions
Outputs:
- attended: bfloat16 [4096, 1024], P(('seq', 'head'))
- grad_queries: bfloat16 [4096, 1024], P(('seq', 'head'))
- grad_keys: bfloat16 [4096, 1024], P(('seq', 'head'))
- grad_values: bfloat16 [4096, 1024], P(('seq', 'head'))
The draws below stay inside these ranges and needn't reach their ends.
Inputs may be any that keep to these rules, and one draw needn't show every extreme that they name: `queries`: Real-valued entries. `keys`: Real-valued entries. `doc_ids`: document ids never fall along the sequence; the longest document holds exactly half of the 4096 tokens.
All inputs are finite; a program needn't handle non-finite values.
Results may differ from the reference program's by a relative error of at most 0.011.
Values may be sent and summed in bfloat16 or wider, within the bound.
No kernel may reach another device: no remote copies, remote signals or barrier semaphores. Data moves between devices by JAX's collectives and lax.ppermute only.
A program may use at most 128 MiB of HBM per device.

```python
import math
import jax
import jax.numpy as jnp
import numpy as np
from jax import lax

HEADS = 16
HEAD_DIM = 64
D = 1024
DOCS = 3
SPARSE = 256
TOKENS = 4096
N_SEQ = 16


def draw_queries(key, part):
    key = jax.random.fold_in(key, 7)
    return jnp.clip(2.5 * jax.random.normal(key, (TOKENS, D), jnp.float32), -10.0, 10.0).astype(jnp.bfloat16)


def draw_keys(key, part):
    key = jax.random.fold_in(key, 13)
    return jnp.clip(jax.random.normal(key, (TOKENS, D), jnp.float32), -6.0, 6.0).astype(jnp.bfloat16)


def level_of(key, dims, cuts, least, high):
    factor_of = 1.0
    for dim, parts in cuts:
        heights = jax.random.uniform(jax.random.fold_in(jax.random.fold_in(key, 6), dim), (parts,), jnp.float32, least / len(cuts), high / len(cuts))
        factor_of = factor_of * jnp.repeat(jnp.exp(heights), dims[dim] // parts).reshape((-1,) + (1,) * (len(dims) - 1 - dim))
    return factor_of


def length_profile(amount, total, reach, slope):
    weights = [(1 << 20) // math.isqrt(rank ** slope) + 1 for rank in range(2, amount + 1)]
    spare, holding = total - reach - (amount - 1), [1] * (amount - 1)
    while spare > 0:
        candidates = [i for i in range(amount - 1) if holding[i] < reach]
        whole, remaining = sum([weights[i] for i in candidates]), spare
        for i in candidates:
            more = min(reach - holding[i], max(1, remaining * weights[i] // whole), spare)
            holding[i] = holding[i] + more
            spare = spare - more
    return np.array([reach] + holding)


def uneven(rng, count, total, bound, skew):
    if count == 2:
        one = jax.random.randint(rng, (), max(1, total - bound), min(bound, total - 1) + 1)
        return jnp.stack([one, total - one])
    lengths = jnp.asarray(length_profile(count, total, bound, skew), jnp.int32)
    pairs = (count - 1) // 2
    source_of, sink = lengths[1:1 + 2 * pairs:2], lengths[2:2 + 2 * pairs:2]
    room = jnp.minimum(source_of - 1, bound - sink)
    moved = jax.random.randint(jax.random.fold_in(rng, 1), (pairs,), 0, 1 << 20) % (room + 1)
    lengths = lengths.at[1:1 + 2 * pairs:2].set(source_of - moved).at[2:2 + 2 * pairs:2].set(sink + moved)
    return lengths[jax.random.permutation(jax.random.fold_in(rng, 2), count)]


def gaussian(key, shape, deviation, reach, pieces=(), held_as=jnp.bfloat16):
    result = deviation * jax.random.normal(key, shape, jnp.float32)
    if pieces:
        result = result * level_of(key, shape, pieces, -0.22, 0.18)
    return jnp.clip(result, -reach, reach).astype(held_as)


def setup_inputs(seed: int = 0) -> dict:
    seeds = jax.random.split(jax.random.key(seed), 6)
    queries = draw_queries(jax.random.fold_in(seeds[5], 71), 0)
    keys = draw_keys(jax.random.fold_in(seeds[5], 71), 0)
    values = gaussian(seeds[2], (TOKENS, D), 1.0, 6.0, ((0, 32),))
    grad_out = gaussian(seeds[3], (TOKENS, D), 1.0, 6.0, ((0, 32),))
    doc_ids = jnp.searchsorted(jnp.cumsum(uneven(seeds[4], DOCS, TOKENS, TOKENS // 2, 0)), jnp.arange(TOKENS), side="right").astype(jnp.int32)
    return dict(queries=queries, keys=keys, values=values, grad_out=grad_out, doc_ids=doc_ids)


def level_rates():
    return [1, 2, 8, N_SEQ]


def visible_mask(segment_docs):
    return segment_docs[:, None] == segment_docs[None, :]


def segment_scores(query_rows, key_rows, segment_docs):
    scores = jnp.dot(query_rows, key_rows.T, preferred_element_type=jnp.float32) * HEAD_DIM ** -0.5
    return jnp.where(visible_mask(segment_docs), scores, -jnp.inf)


def segment_forward(segment_args):
    query_rows, key_rows, value_rows, segment_docs = segment_args
    scores = segment_scores(query_rows, key_rows, segment_docs)
    row_max = jnp.max(scores, axis=1)
    weights = jnp.exp(scores - row_max[:, None])
    row_total = jnp.sum(weights, axis=1)
    summed = jnp.dot(weights.astype(jnp.bfloat16), value_rows, preferred_element_type=jnp.float32)
    return row_max, row_total, summed


def segment_backward(segment_args):
    query_rows, key_rows, value_rows, upstream_rows, segment_docs, log_total, row_delta = segment_args
    scale = HEAD_DIM ** -0.5
    scores = segment_scores(query_rows, key_rows, segment_docs)
    probability = jnp.exp(scores - log_total[:, None])
    grad_values = jnp.dot(probability.astype(jnp.bfloat16).T, upstream_rows, preferred_element_type=jnp.float32)
    grad_scores = jnp.dot(upstream_rows, value_rows.T, preferred_element_type=jnp.float32)
    shifted = (probability * (grad_scores - row_delta[:, None])).astype(jnp.bfloat16)
    grad_queries = jnp.dot(shifted, key_rows, preferred_element_type=jnp.float32) * scale
    grad_keys = jnp.dot(shifted.T, query_rows, preferred_element_type=jnp.float32) * scale
    return grad_queries, grad_keys, grad_values


def reference(queries, keys, values, grad_out, doc_ids):
    attended_cols, query_cols, key_cols, value_cols = [], [], [], []
    for head_id in range(HEADS):
        columns = slice(head_id * HEAD_DIM, (head_id + 1) * HEAD_DIM)
        head_query = queries[:, columns]
        head_key = keys[:, columns]
        head_value = values[:, columns]
        head_upstream = grad_out[:, columns]
        row_max = jnp.full((TOKENS,), -jnp.inf, jnp.float32)
        row_total = jnp.zeros((TOKENS,), jnp.float32)
        summed = jnp.zeros((TOKENS, HEAD_DIM), jnp.float32)
        for dilation in level_rates():
            picked = slice(head_id % dilation, None, dilation)
            stats = lax.map(segment_forward, (
                head_query[picked].reshape(-1, SPARSE, HEAD_DIM),
                head_key[picked].reshape(-1, SPARSE, HEAD_DIM),
                head_value[picked].reshape(-1, SPARSE, HEAD_DIM),
                doc_ids[picked].reshape(-1, SPARSE)))
            level_max = stats[0].reshape(-1)
            level_total = stats[1].reshape(-1)
            level_sum = stats[2].reshape(-1, HEAD_DIM)
            old_max = row_max[picked]
            new_max = jnp.maximum(old_max, level_max)
            old_scale = jnp.exp(old_max - new_max)
            new_scale = jnp.exp(level_max - new_max)
            row_total = row_total.at[picked].set(row_total[picked] * old_scale + level_total * new_scale)
            summed = summed.at[picked].set(summed[picked] * old_scale[:, None] + level_sum * new_scale[:, None])
            row_max = row_max.at[picked].set(new_max)
        output = summed / row_total[:, None]
        log_total = row_max + jnp.log(row_total)
        row_delta = jnp.sum(head_upstream.astype(jnp.float32) * output, axis=1)
        grad_query = jnp.zeros((TOKENS, HEAD_DIM), jnp.float32)
        grad_key = jnp.zeros((TOKENS, HEAD_DIM), jnp.float32)
        grad_value = jnp.zeros((TOKENS, HEAD_DIM), jnp.float32)
        for dilation in level_rates():
            picked = slice(head_id % dilation, None, dilation)
            grads = lax.map(segment_backward, (
                head_query[picked].reshape(-1, SPARSE, HEAD_DIM),
                head_key[picked].reshape(-1, SPARSE, HEAD_DIM),
                head_value[picked].reshape(-1, SPARSE, HEAD_DIM),
                head_upstream[picked].reshape(-1, SPARSE, HEAD_DIM),
                doc_ids[picked].reshape(-1, SPARSE),
                log_total[picked].reshape(-1, SPARSE),
                row_delta[picked].reshape(-1, SPARSE)))
            grad_query = grad_query.at[picked].add(grads[0].reshape(-1, HEAD_DIM))
            grad_key = grad_key.at[picked].add(grads[1].reshape(-1, HEAD_DIM))
            grad_value = grad_value.at[picked].add(grads[2].reshape(-1, HEAD_DIM))
        attended_cols.append(output.astype(jnp.bfloat16))
        query_cols.append(grad_query.astype(jnp.bfloat16))
        key_cols.append(grad_key.astype(jnp.bfloat16))
        value_cols.append(grad_value.astype(jnp.bfloat16))
    return (jnp.concatenate(attended_cols, axis=1), jnp.concatenate(query_cols, axis=1),
            jnp.concatenate(key_cols, axis=1), jnp.concatenate(value_cols, axis=1))
```

```python
import dataclasses
import functools

import jax
import jax.numpy as jnp
from jax import lax
from jax.experimental import pallas as pl
from jax.experimental.pallas import tpu as pltpu
from jax.sharding import PartitionSpec as P

HEAD_DIM = 64
LANES = 2 * HEAD_DIM
HIDDEN = -131072.0
DOC_LANE, TOTAL_LANE, QUERY_PAD, KEY_PAD = HEAD_DIM, HEAD_DIM + 3, HEAD_DIM + 6, HEAD_DIM + 7
QUERY_TILE = 256
FAR_ROWS = 8
COPY_PARTS = 2
PACK_LIMIT = 56 * 1024 * 1024
VMEM_LIMIT = 14 * 1024 * 1024


def dot(a, b, contract):
    return lax.dot_general(a, b, ((contract[:1], contract[1:]), ((), ())), preferred_element_type=jnp.float32)


def row_order(rows, rates, shape, axis):
    row = lax.broadcasted_iota(jnp.int32, shape, axis)
    order = row * rates[-1]
    for rate, above in zip(rates[-2::-1], rates[:0:-1]):
        between, fresh = above // rate - 1, row - rows // above
        if between > 0:
            group = fresh if between == 1 else lax.div(fresh, between)
            order = jnp.where(fresh >= 0, group * above + (fresh - group * between + 1) * rate, order)
    return order


def lane_of(shape):
    return lax.broadcasted_iota(jnp.int32, shape, 1)


def halves_swapped(x):
    return jnp.concatenate([x[:, HEAD_DIM:], x[:, :HEAD_DIM]], axis=1)


def lane_mask(rows, at_low, at_high):
    return jnp.where(lane_of((rows, LANES)) < HEAD_DIM, at_low, at_high).astype(jnp.bfloat16)


def pack_kernel(rates, q_hbm, k_hbm, v_hbm, g_hbm, out_hbm, q_ref, k_ref, v_ref, g_ref, out_ref, arrived, left):
    rows, width = q_ref.shape
    copies, outgoing = [], []
    for part in range(COPY_PARTS):
        cols = pl.ds(part * (width // COPY_PARTS), width // COPY_PARTS)
        held = ((q_hbm, q_ref), (k_hbm, k_ref), (v_hbm, v_ref), (g_hbm, g_ref))
        copies.append(
            [pltpu.make_async_copy(a.at[:, cols], b.at[:, cols], arrived.at[part, i]) for i, (a, b) in enumerate(held)]
        )
    for part in copies:
        for copy in part:
            copy.start()
    order = row_order(rows, rates, (rows, rows), 0)
    lane = lane_of((rows, rows))
    low, high = lane_mask(rows, 1.0, 0.0), lane_mask(rows, 0.0, 1.0)
    for tile in range(width // LANES):
        cols = slice(tile * LANES, (tile + 1) * LANES)
        part, inside = divmod(tile * LANES, width // COPY_PARTS)
        if inside == 0:
            for copy in copies[part]:
                copy.wait()
        pairs = ((q_ref[:, cols], g_ref[:, cols]), (k_ref[:, cols], v_ref[:, cols]))
        even = [first * low + halves_swapped(second) * high for first, second in pairs]
        odd = [halves_swapped(first) * low + second * high for first, second in pairs]
        for side, sources in enumerate((even, odd)):
            pick = jnp.where(order == ((lane - (2 * tile + side)) & (rows - 1)), 1.0, 0.0).astype(jnp.bfloat16)
            moved = dot(pick, jnp.concatenate(sources, axis=1), (1, 0)).astype(jnp.bfloat16)
            out_ref[2 * tile + side, 0] = moved[:, :LANES]
            out_ref[2 * tile + side, 1] = moved[:, LANES:]
        if inside + LANES == width // COPY_PARTS:
            done = pl.ds(part * (width // HEAD_DIM // COPY_PARTS), width // HEAD_DIM // COPY_PARTS)
            outgoing.append(pltpu.make_async_copy(out_ref.at[done], out_hbm.at[done], left.at[part]))
            outgoing[-1].start()
    for copy in outgoing:
        copy.wait()


def unpack_kernel(rates, in_ref, *refs):
    (out_hbm, dq_hbm, dk_hbm, dv_hbm), (out_ref, dq_ref, dk_ref, dv_ref, left) = refs[:4], refs[4:]
    rows, width = out_ref.shape
    outgoing = []
    order = row_order(rows, rates, (rows, rows), 1)
    token = lax.broadcasted_iota(jnp.int32, (rows, rows), 0)
    low, high = lane_mask(rows, 1.0, 0.0), lane_mask(rows, 0.0, 1.0)
    for tile in range(width // LANES):
        cols = slice(tile * LANES, (tile + 1) * LANES)
        picks, sources = [], []
        for side in range(2):
            head = 2 * tile + side
            picks.append(jnp.where(((order + head) & (rows - 1)) == token, 1.0, 0.0).astype(jnp.bfloat16))
            columns = []
            for kind in range(2):
                x = in_ref[head, kind]
                y = halves_swapped(x)
                columns += [y * high, x * high] if side else [x * low, y * low]
            sources.append(jnp.concatenate(columns, axis=1))
        moved = dot(jnp.concatenate(picks, axis=1), jnp.concatenate(sources, axis=0), (1, 0)).astype(jnp.bfloat16)
        for i, ref in enumerate((dq_ref, out_ref, dk_ref, dv_ref)):
            ref[:, cols] = moved[:, i * LANES : (i + 1) * LANES]
        part, inside = divmod((tile + 1) * LANES, width // COPY_PARTS)
        if inside == 0:
            done = pl.ds((part - 1) * (width // COPY_PARTS), width // COPY_PARTS)
            held = ((out_ref, out_hbm), (dq_ref, dq_hbm), (dk_ref, dk_hbm), (dv_ref, dv_hbm))
            for i, (a, b) in enumerate(held):
                outgoing.append(pltpu.make_async_copy(a.at[:, done], b.at[:, done], left.at[part - 1, i]))
                outgoing[-1].start()
    for copy in outgoing:
        copy.wait()


@dataclasses.dataclass(frozen=True)
class Plan:
    heads: int
    rows: int
    rates: tuple
    near: tuple
    far: tuple

    @property
    def late(self):
        return self.near[2:], max([count for count, _ in self.near[2:]] + [held for _, held, _ in self.far])


def plan_of(rows, width, shards, parts):
    heads, rates = width // HEAD_DIM, (1, 2, 8, shards)
    near, far = [], []
    for rate in rates:
        span = rows * parts * rate
        if span <= rows * heads:
            near.append((rows // rate, span // rows))
        else:
            far.append((rows // rate, max(rows // rate, FAR_ROWS), span // (rows * heads)))
    return Plan(heads, rows, rates, tuple(near), tuple(far))


def my_place(heads):
    index = lax.axis_index("seq") * lax.axis_size("head") + lax.axis_index("head")
    return lax.div(index, heads), index & (heads - 1)


def rows_of(ref, blocks, count):
    if count == ref.shape[1]:
        return ref[blocks.start : blocks.stop].reshape(len(blocks) * count, LANES)
    if ref.dtype == jnp.bfloat16 and count % 16:
        held = -(-count // 16) * 16
        parts = [ref[j, 0:held].astype(jnp.float32)[0:count] for j in blocks]
        return jnp.concatenate(parts, axis=0).astype(jnp.bfloat16)
    return jnp.concatenate([ref[j, 0:count] for j in blocks], axis=0)


def set_rows(ref, blocks, count, value):
    for i, j in enumerate(blocks):
        ref[j, 0:count] = value[i * count : (i + 1) * count]


def add_rows(ref, blocks, count, value):
    set_rows(ref, blocks, count, rows_of(ref, blocks, count) + value)


def doc_lanes(doc_ref, rows):
    docs = doc_ref[...]
    first, second = [jnp.sum(jnp.where(docs < d, 1, 0)) for d in (1, 2)]
    lane, last = lane_of((rows, LANES)), jnp.iinfo(jnp.int32).max
    start, stop = jnp.full((rows, LANES), last, jnp.int32), jnp.full((rows, LANES), 0, jnp.int32)
    for at, lo, hi in ((0, 0, first), (1, first, second), (2, second, last), (KEY_PAD - DOC_LANE, 0, last)):
        start = jnp.where(lane == DOC_LANE + at, lo, start)
        stop = jnp.where(lane == DOC_LANE + at, hi, stop)
    return start, stop


def key_lanes(marked, lane, padding):
    outside = jnp.where((lane >= TOTAL_LANE) & (lane <= QUERY_PAD), 1.0, 0.0)
    outside = jnp.where((lane >= DOC_LANE) & (lane < TOTAL_LANE), HIDDEN, outside)
    value = jnp.where(marked, 0.0, outside)
    if padding is not None:
        value = jnp.where((lane == KEY_PAD) & padding, HIDDEN, value)
    return value.astype(jnp.bfloat16)


def far_operands(plan, level, doc_ref, qa, ka, va, far_ref):
    count, held, chunks = plan.far[level]
    heads, rows = plan.heads, plan.rows
    chunk, head = my_place(heads)
    every, shape = range(heads), (heads * held, LANES)
    lane, index = lane_of(shape), lax.broadcasted_iota(jnp.int32, shape, 0)
    low, high = lane_mask(shape[0], 1.0, 0.0), lane_mask(shape[0], 0.0, 1.0)
    padding = None if count == held else (index & (held - 1)) >= count
    queries = rows_of(qa, every, held)
    key_sets, value_sets = [rows_of(ka, every, held)], [rows_of(va, every, held)]
    if padding is not None:
        queries = jnp.where((lane == QUERY_PAD) & padding, HIDDEN, queries.astype(jnp.float32)).astype(jnp.bfloat16)
        own = jnp.where((lane == KEY_PAD) & padding, HIDDEN, key_sets[0].astype(jnp.float32))
        key_sets[0] = own.astype(jnp.bfloat16)
    start, stop = doc_lanes(doc_ref, shape[0])
    order = row_order(rows, plan.rates, (held, LANES), 0)
    spots = jnp.concatenate([(order + head) & (rows - 1)] * heads, axis=0)
    for i in range(1, chunks):
        token = ((chunk ^ i) * heads + lax.div(index, held)) * rows + spots
        marked = (token >= start) & (token < stop)
        key_sets.append(far_ref[i - 1] * low + key_lanes(marked, lane, padding))
        value_sets.append(far_ref[i - 1] * high + low)
    return queries, jnp.concatenate(key_sets, axis=0), jnp.concatenate(value_sets, axis=0)


def forward(queries, keys, values):
    scores = dot(queries, keys, (1, 1))
    peak = jnp.max(scores, axis=1, keepdims=True)
    weights = jnp.exp(scores - peak).astype(jnp.bfloat16)
    return jnp.broadcast_to(peak, (queries.shape[0], LANES)), dot(weights, values, (1, 0))


def backward(queries, upstream, keys, values):
    probability = jnp.exp(dot(keys, queries, (1, 1)))
    shifted = (probability * dot(values, upstream, (1, 1))).astype(jnp.bfloat16)
    for_keys = dot(shifted, queries, (1, 0))
    for_values = dot(probability.astype(jnp.bfloat16), upstream, (1, 0))
    key_low = lane_of(for_keys.shape) < HEAD_DIM
    return dot(shifted, keys, (0, 0)), jnp.where(key_low, for_keys, for_values)


def merged(old_peak, old, peak, summed):
    new_peak = jnp.maximum(old_peak, peak)
    return new_peak, old * jnp.exp(old_peak - new_peak) + summed * jnp.exp(peak - new_peak)


def tiles(plan, count, span):
    per_tile = max(1, QUERY_TILE // count)
    for start in range(0, plan.heads, span):
        for begin in range(start, start + span, per_tile):
            yield range(start, start + span), range(begin, min(begin + per_tile, start + span))


def near_kernel(plan, doc_ref, x_ref, qa, ka, va, ga, acc, top):
    heads, rows = plan.heads, plan.rows
    chunk, head = my_place(heads)
    lane = lane_of((rows, LANES))
    spot = (row_order(rows, plan.rates, (rows, LANES), 0) + head) & (rows - 1)
    start, stop = doc_lanes(doc_ref, rows)
    low, high = lane_mask(rows, 1.0, 0.0), lane_mask(rows, 0.0, 1.0)
    low_scaled = lane_mask(rows, HEAD_DIM**-0.5, 0.0)
    for j in range(heads):
        token = (chunk * heads + j) * rows + spot
        marked = (token >= start) & (token < stop)
        qg, kv = x_ref[j, 0], x_ref[j, 1]
        qa[j] = qg * low_scaled + jnp.where(marked, 1.0, 0.0).astype(jnp.bfloat16)
        ka[j] = kv * low + key_lanes(marked, lane, None)
        va[j] = kv * high + low
        ga[j] = qg * high
    for level, (count, span) in enumerate(plan.near):
        for key_blocks, blocks in tiles(plan, count, span):
            peak, summed = forward(*(rows_of(r, b, count) for r, b in ((qa, blocks), (ka, key_blocks), (va, key_blocks))))
            if level > 0:
                peak, summed = merged(rows_of(top, blocks, count), rows_of(acc, blocks, count), peak, summed)
            set_rows(top, blocks, count, peak)
            set_rows(acc, blocks, count, summed)


def pieces(x):
    first = x.astype(jnp.bfloat16).astype(jnp.float32)
    second = (x - first).astype(jnp.bfloat16).astype(jnp.float32)
    return first, second, x - first - second


def in_lanes(x, at):
    first, second, third = pieces(x)
    lane = lane_of(x.shape)
    value = jnp.where(lane == at, first, jnp.where(lane == at + 1, second, jnp.where(lane == at + 2, third, 0.0)))
    return value.astype(jnp.bfloat16)


def far_kernel(plan, doc_ref, qa, ka, va, ga, acc_in, top_in, *refs):
    levels = len(plan.far)
    far_in, refs = refs[:levels], refs[levels:]
    (qb, gb, output), refs = refs[:3], refs[3:]
    far_dq, far_dkv, far_out, (acc, top) = refs[:levels], refs[levels : 2 * levels], refs[2 * levels : -2], refs[-2:]
    heads, rows = plan.heads, plan.rows
    every = range(heads)
    _, reach = plan.late
    for j in every:
        acc[j], top[j] = acc_in[j, 0:reach], top_in[j, 0:reach]
    for level, (_, held, _) in enumerate(plan.far):
        peak, summed = forward(*far_operands(plan, level, doc_ref, qa, ka, va, far_in[level]))
        peak, summed = merged(rows_of(top, every, held), rows_of(acc, every, held), peak, summed)
        set_rows(top, every, held, peak)
        set_rows(acc, every, held, summed)

    low = lane_of((rows, LANES)) < HEAD_DIM
    for j in every:
        summed = jnp.concatenate([acc[j], acc_in[j, reach:]], axis=0)
        peak = jnp.concatenate([top[j], top_in[j, reach:]], axis=0)
        total = jnp.where(low, summed, pltpu.roll(summed, HEAD_DIM, 1))
        normal = summed / total
        upstream = ga[j]
        delta = jnp.sum(normal * upstream.astype(jnp.float32), axis=1, keepdims=True)
        qb[j] = qa[j] + in_lanes(-(peak + jnp.log(total)), TOTAL_LANE)
        gb[j] = upstream + in_lanes(jnp.broadcast_to(-delta, (rows, LANES)), 0)
        output[j] = normal

    for level, (_, held, chunks) in enumerate(plan.far):
        queries, keys, values = far_operands(plan, level, doc_ref, qb, ka, va, far_in[level])
        for_queries, for_keys = backward(queries, rows_of(gb, every, held), keys, values)
        size = heads * held
        far_dq[level][...] = for_queries
        far_dkv[level][...] = for_keys[:size]
        for i in range(1, chunks):
            far_out[level][i - 1] = for_keys[i * size : (i + 1) * size].astype(jnp.bfloat16)


def local_kernel(plan, qb, ka, va, gb, dq, dkv):
    for level, (count, span) in enumerate(plan.near[:2]):
        for key_blocks, blocks in tiles(plan, count, span):
            for_queries, for_keys = backward(
                *(rows_of(r, b, count) for r, b in ((qb, blocks), (gb, blocks), (ka, key_blocks), (va, key_blocks)))
            )
            (add_rows if level else set_rows)(dq, blocks, count, for_queries)
            fresh = level == 0 and blocks.start == key_blocks.start
            (set_rows if fresh else add_rows)(dkv, key_blocks, count, for_keys)


def last_kernel(plan, qb, ka, va, gb, output, dq_in, dkv_in, *refs):
    levels = len(plan.far)
    far_dq, far_dkv, far_back = refs[:levels], refs[levels : 2 * levels], refs[2 * levels : 3 * levels]
    out_ref, dq, dkv = refs[3 * levels :]
    heads, rows = plan.heads, plan.rows
    every, (near, reach) = range(heads), plan.late
    for j in every:
        dq[j], dkv[j] = dq_in[j, 0:reach], dkv_in[j, 0:reach]
    for count, span in near:
        for key_blocks, blocks in tiles(plan, count, span):
            for_queries, for_keys = backward(
                *(rows_of(r, b, count) for r, b in ((qb, blocks), (gb, blocks), (ka, key_blocks), (va, key_blocks)))
            )
            add_rows(dq, blocks, count, for_queries)
            add_rows(dkv, key_blocks, count, for_keys)
    for level, (_, held, chunks) in enumerate(plan.far):
        add_rows(dq, every, held, far_dq[level][...])
        partial = far_dkv[level][...]
        for i in range(1, chunks):
            partial = partial + far_back[level][i - 1].astype(jnp.float32)
        add_rows(dkv, every, held, partial)
    low = lane_of((rows, LANES)) < HEAD_DIM
    for j in every:
        for_queries = jnp.concatenate([dq[j], dq_in[j, reach:]], axis=0)
        out_ref[j, 0] = jnp.where(low, for_queries * HEAD_DIM**-0.5, output[j]).astype(jnp.bfloat16)
        out_ref[j, 1] = jnp.concatenate([dkv[j], dkv_in[j, reach:]], axis=0).astype(jnp.bfloat16)


def landed(x):
    return pltpu.VMEM(x.shape, x.dtype)


def call(kernel, out_shapes, args, scratch=(), flops=0, inputs=pltpu.VMEM, outputs=pltpu.VMEM, limit=VMEM_LIMIT):
    moved = sum(x.size * x.dtype.itemsize for x in (*args, *out_shapes))
    return pl.pallas_call(
        kernel,
        out_shape=out_shapes,
        in_specs=[pl.BlockSpec(memory_space=inputs)] * len(args),
        out_specs=[pl.BlockSpec(memory_space=outputs)] * len(out_shapes),
        scratch_shapes=scratch,
        compiler_params=pltpu.CompilerParams(vmem_limit_bytes=limit),
        cost_estimate=pl.CostEstimate(flops=flops, bytes_accessed=moved, transcendentals=0),
    )(*args)


def body(queries, keys, values, grad_out, doc_ids):
    rows, width = queries.shape
    shards, parts = lax.axis_size("seq"), lax.axis_size("head")
    devices, axes = shards * parts, ("seq", "head")
    plan = plan_of(rows, width, shards, parts)
    heads, _, (_, reach) = plan.heads, plan.far, plan.late
    groups = [[c * heads + h for h in range(heads)] for c in range(devices // heads)]

    def exchange(x):
        return lax.all_to_all(x, axes, 0, 0, axis_index_groups=groups, tiled=True)

    def from_chunk(x, i):
        return lax.ppermute(x, axes, [(d, d ^ (i * heads)) for d in range(devices)])

    def run(kernel, *rest, **more):
        return call(functools.partial(kernel, plan), *rest, **more)

    shape, low, full = jax.ShapeDtypeStruct, jnp.bfloat16, jnp.float32
    packed = shape((heads, 2, rows, LANES), low)
    operand, total = shape((heads, rows, LANES), low), shape((heads, rows, LANES), full)
    prefix = shape((heads, reach, LANES), full)
    own_far = [shape((heads * held, LANES), full) for _, held, _ in plan.far]
    docs = doc_ids.reshape(-1, LANES)

    inputs = (queries, keys, values, grad_out)
    semaphores = pltpu.SemaphoreType.DMA((COPY_PARTS, len(inputs)))
    landing = [landed(x) for x in (*inputs, packed)] + [semaphores, pltpu.SemaphoreType.DMA((COPY_PARTS,))]
    mine = call(
        functools.partial(pack_kernel, plan.rates), [packed], inputs, landing, flops=1 << 27, inputs=pltpu.HBM, outputs=pltpu.HBM, limit=PACK_LIMIT
    )[0]
    chunk = exchange(mine)
    gathered = []
    for _, held, chunks in plan.far:
        picked = chunk[:, 1, :held].reshape(heads * held, LANES)
        gathered.append(jnp.stack([from_chunk(picked, i) for i in range(1, chunks)]))
    qa, ka, va, ga, acc, top = run(near_kernel, [operand] * 4 + [total] * 2, (docs, chunk), flops=1 << 30)
    sent = [shape(x.shape, x.dtype) for x in gathered]
    qb, gb, output, *rest = run(
        far_kernel,
        [operand] * 2 + [total] + own_far * 2 + sent,
        (docs, qa, ka, va, ga, acc, top, *gathered),
        [landed(prefix)] * 2,
        flops=1 << 28,
    )
    owned, partials = rest[: 2 * len(plan.far)], rest[2 * len(plan.far) :]
    returned = [jnp.stack([from_chunk(x[i], i + 1) for i in range(x.shape[0])]) for x in partials]
    dq, dkv = run(local_kernel, [total] * 2, (qb, ka, va, gb), flops=1 << 30)
    grads = run(
        last_kernel, [packed], (qb, ka, va, gb, output, dq, dkv, *owned, *returned), [landed(prefix)] * 2, flops=1 << 28
    )[0]
    result = [shape((rows, width), low)] * 4
    leaving = [landed(x) for x in result] + [semaphores]
    unpack = functools.partial(unpack_kernel, plan.rates)
    return tuple(call(unpack, result, (exchange(grads),), leaving, flops=1 << 27, outputs=pltpu.HBM))


def solution(mesh):
    split = P(("seq", "head"), None)
    return jax.shard_map(
        body, mesh=mesh, in_specs=(split,) * 4 + (P(),), out_specs=(split,) * 4, check_vma=False
    )
```

```python
import dataclasses
import functools

import jax
import jax.numpy as jnp
from jax import lax
from jax.experimental import pallas as pl
from jax.experimental.pallas import tpu as pltpu
from jax.sharding import PartitionSpec as P

HEAD_DIM = 64
LANES = 2 * HEAD_DIM
HIDDEN = -131072.0
DOC_LANE, TOTAL_LANE, QUERY_PAD, KEY_PAD = HEAD_DIM, HEAD_DIM + 3, HEAD_DIM + 6, HEAD_DIM + 7
QUERY_TILE = 256
FAR_ROWS = 8
PACK_LIMIT = 56 * 1024 * 1024
VMEM_LIMIT = 14 * 1024 * 1024


def dot(a, b, contract):
    return lax.dot_general(a, b, ((contract[:1], contract[1:]), ((), ())), preferred_element_type=jnp.float32)


def row_order(rows, rates, shape, axis):
    row = lax.broadcasted_iota(jnp.int32, shape, axis)
    order = row * rates[-1]
    for rate, above in zip(rates[-2::-1], rates[:0:-1]):
        between, fresh = above // rate - 1, row - rows // above
        if between > 0:
            group = fresh if between == 1 else lax.div(fresh, between)
            order = jnp.where(fresh >= 0, group * above + (fresh - group * between + 1) * rate, order)
    return order


def lane_of(shape):
    return lax.broadcasted_iota(jnp.int32, shape, 1)


def halves_swapped(x):
    return jnp.concatenate([x[:, HEAD_DIM:], x[:, :HEAD_DIM]], axis=1)


def lane_mask(rows, at_low, at_high):
    return jnp.where(lane_of((rows, LANES)) < HEAD_DIM, at_low, at_high).astype(jnp.float32).astype(jnp.bfloat16)


@dataclasses.dataclass(frozen=True)
class Plan:
    heads: int
    rows: int
    rates: tuple
    near: tuple
    far: tuple

    bit: int

    @property
    def reach(self):
        return max([16] + [held for _, held, _ in self.far] + [count for count, _ in self.near[2:]])

    @property
    def group(self):
        return max(2 * self.bit, self.near[1][1])

    def group_order(self, base):
        return [m for m in self.order if base <= m < base + self.group]

    @property
    def others(self):
        return max([chunks for _, _, chunks in self.far], default=1) - 1

    @property
    def message(self):
        return 2 * self.rows + self.others * self.reach

    @property
    def steps(self):
        return [m for m in range(self.heads) if not m & self.bit]

    @property
    def order(self):
        every = self.steps[-1]
        pairs = [(every ^ m, m) for m in self.steps[1:-1] if m < every ^ m]
        return [every, *(m for pair in pairs for m in pair), 0]

    def far_place(self, i):
        return 2 * self.rows + (i - 1) * self.reach


def plan_of(rows, width, shards, parts):
    heads, rates = width // HEAD_DIM, (1, 2, 8, shards)
    near, far = [], []
    for rate in rates:
        span = rows * parts * rate
        if span <= rows * heads:
            near.append((rows // rate, span // rows))
        else:
            far.append((rows // rate, max(rows // rate, FAR_ROWS), span // (rows * heads)))
    return Plan(heads, rows, rates, tuple(near), tuple(far), parts)


def my_place(heads):
    index = lax.axis_index("seq") * lax.axis_size("head") + lax.axis_index("head")
    return lax.div(index, heads), index & (heads - 1)


def pack_pair(plan, step, columns, blocks, far):
    rows = plan.rows
    _, me = my_place(plan.heads)
    order = row_order(rows, plan.rates, (rows, rows), 0)
    lane = lane_of((rows, rows))
    low, high = lane_mask(rows, 1.0, 0.0), lane_mask(rows, 0.0, 1.0)
    q, k, v, g = columns
    for side in range(2):
        if side:
            sources = [halves_swapped(first) * low + second * high for first, second in ((q, g), (k, v))]
        else:
            sources = [first * low + halves_swapped(second) * high for first, second in ((q, g), (k, v))]
        head = (me ^ step) & ~1 | side
        pick = jnp.where(order == ((lane - head) & (rows - 1)), 1.0, 0.0).astype(jnp.bfloat16)
        moved = dot(pick, jnp.concatenate(sources, axis=1), (1, 0)).astype(jnp.bfloat16)
        slot = plan.steps.index(step & ~plan.bit) + ((me & 1) ^ side)
        blocks[slot, 0:rows] = moved[:, :LANES]
        blocks[slot, rows : 2 * rows] = moved[:, LANES:]
        far[slot] = moved[: plan.reach, LANES:]


def tile_of(plan, step):
    _, me = my_place(plan.heads)
    return pl.ds(pl.multiple_of(((me ^ step) >> 1) * LANES, LANES), LANES)


def send_kernel(plan, *refs):
    inputs, (blocks, far, held, arrived) = refs[:4], refs[4:]
    steps = [step | plan.bit for step in plan.steps[::2]]
    copies = []
    for n, step in enumerate(steps):
        cols = tile_of(plan, step)
        copies.append(
            [pltpu.make_async_copy(x.at[:, cols], held.at[n, i], arrived.at[n, i]) for i, x in enumerate(inputs)]
        )
        for copy in copies[-1]:
            copy.start()
    for n, step in enumerate(steps):
        for copy in copies[n]:
            copy.wait()
        pack_pair(plan, step, [held[n, i] for i in range(4)], blocks, far)


def keep_kernel(plan, *refs):
    inputs, (blocks, far) = refs[:4], refs[4:]
    for step in plan.steps[::2]:
        cols = tile_of(plan, step)
        pack_pair(plan, step, [x[:, cols] for x in inputs], blocks, far)


def join_kernel(plan, keep, received, *refs):
    same, cross, messages = refs[: plan.others], refs[plan.others : 2 * plan.others], refs[2 * plan.others :]
    for step, message in zip(plan.order, messages):
        slot = plan.steps.index(step)
        for half, (block, far) in enumerate(((keep, same), (received, cross))):
            message[half, 0 : 2 * plan.rows] = block[slot]
            for i in range(1, plan.others + 1):
                at = plan.far_place(i)
                message[half, at : at + plan.reach] = far[i - 1][slot]


def part_kernel(plan, *refs):
    steps = len(plan.steps)
    messages, send, refs = refs[:steps], refs[steps], refs[steps + 1 :]
    same, cross = refs[: plan.others], refs[plan.others :]
    for step, message in zip(plan.order, messages):
        slot = plan.steps.index(step)
        send[slot] = message[1, 0 : 2 * plan.rows]
        for i in range(1, plan.others + 1):
            at = plan.far_place(i)
            same[i - 1][slot] = message[0, at : at + plan.reach]
            cross[i - 1][slot] = message[1, at : at + plan.reach]


def unpack_kernel(plan, *refs):
    steps, others = len(plan.steps), plan.others
    messages, received, refs = refs[:steps], refs[steps], refs[steps + 1 :]
    same, cross, (out_ref, dq_ref, dk_ref, dv_ref) = refs[:others], refs[others : 2 * others], refs[2 * others :]
    rows, width = out_ref.shape
    _, me = my_place(plan.heads)
    order = row_order(rows, plan.rates, (rows, rows), 1)
    token = lax.broadcasted_iota(jnp.int32, (rows, rows), 0)
    masks = []
    for distance in range(2):
        side = (me & 1) ^ distance
        masks.append((lane_mask(rows, 1 - side, 0), lane_mask(rows, 0, side)))
    for step in range(0, plan.heads, 2):
        tile = (me ^ step) >> 1
        cols = pl.ds(pl.multiple_of(tile * LANES, LANES), LANES)
        picks, sources = [], []
        for distance in range(2):
            slot = plan.steps.index(step & ~plan.bit) + distance
            block, far = (received.at[slot], cross) if step & plan.bit else (messages[plan.order.index(plan.steps[slot])].at[0], same)
            x, kv = block[0:rows], block[rows : 2 * rows]
            first = kv[: plan.reach].astype(jnp.float32)
            for ref in far:
                first = first + ref[slot].astype(jnp.float32)
            kv = jnp.concatenate([first.astype(jnp.bfloat16), kv[plan.reach :]], axis=0)
            at_low, at_high = masks[distance]
            columns = []
            for y in (x, kv):
                turned = halves_swapped(y)
                columns += [y * at_low + turned * at_high, turned * at_low + y * at_high]
            picks.append(jnp.where(((order + (me ^ (step + distance))) & (rows - 1)) == token, 1.0, 0.0).astype(jnp.bfloat16))
            sources.append(jnp.concatenate(columns, axis=1))
        moved = dot(jnp.concatenate(picks, axis=1), jnp.concatenate(sources, axis=0), (1, 0)).astype(jnp.bfloat16)
        for i, ref in enumerate((dq_ref, out_ref, dk_ref, dv_ref)):
            ref[:, cols] = moved[:, i * LANES : (i + 1) * LANES]


def rows_of(ref, blocks, count):
    if count == ref.shape[1] and count % 16 == 0:
        return ref[blocks.start : blocks.stop].reshape(len(blocks) * count, LANES)
    if ref.dtype == jnp.bfloat16 and count % 16:
        held = -(-count // 16) * 16
        parts = [ref[j, 0:held].astype(jnp.float32)[0:count] for j in blocks]
        return jnp.concatenate(parts, axis=0).astype(jnp.bfloat16)
    return jnp.concatenate([ref[j, 0:count] for j in blocks], axis=0)


def rows_among(refs, every, count):
    size = refs[0].shape[0]
    return jnp.concatenate([rows_of(refs[j // size], range(j % size, j % size + 1), count) for j in every], axis=0)


def set_rows(ref, blocks, count, value):
    for i, j in enumerate(blocks):
        ref[j, 0:count] = value[i * count : (i + 1) * count]


def add_rows(ref, blocks, count, value):
    set_rows(ref, blocks, count, rows_of(ref, blocks, count) + value)


def doc_lanes(doc_ref, rows):
    docs = doc_ref[...]
    first, second = [jnp.sum(jnp.where(docs < d, 1, 0)) for d in (1, 2)]
    lane, last = lane_of((rows, LANES)), jnp.iinfo(jnp.int32).max
    start, stop = jnp.full((rows, LANES), last, jnp.int32), jnp.full((rows, LANES), 0, jnp.int32)
    for at, lo, hi in ((0, 0, first), (1, first, second), (2, second, last), (KEY_PAD - DOC_LANE, 0, last)):
        start = jnp.where(lane == DOC_LANE + at, lo, start)
        stop = jnp.where(lane == DOC_LANE + at, hi, stop)
    return start, stop


def key_lanes(marked, lane, padding):
    outside = jnp.where((lane >= TOTAL_LANE) & (lane <= QUERY_PAD), 1.0, 0.0)
    outside = jnp.where((lane >= DOC_LANE) & (lane < TOTAL_LANE), HIDDEN, outside)
    value = jnp.where(marked, 0.0, outside)
    if padding is not None:
        value = jnp.where((lane == KEY_PAD) & padding, HIDDEN, value)
    return value.astype(jnp.bfloat16)


def far_operands(plan, level, doc_ref, qa, ka, va, block_of):
    count, held, chunks = plan.far[level]
    heads, rows = plan.heads, plan.rows
    chunk, head = my_place(heads)
    every, shape = range(heads), (heads * held, LANES)
    lane, index = lane_of(shape), lax.broadcasted_iota(jnp.int32, shape, 0)
    low, high = lane_mask(shape[0], 1.0, 0.0), lane_mask(shape[0], 0.0, 1.0)
    padding = None if count == held else (index & (held - 1)) >= count
    queries = rows_among(qa, every, held)
    key_sets, value_sets = [rows_among(ka, every, held)], [rows_among(va, every, held)]
    if padding is not None:
        queries = jnp.where((lane == QUERY_PAD) & padding, HIDDEN, queries.astype(jnp.float32)).astype(jnp.bfloat16)
        own = jnp.where((lane == KEY_PAD) & padding, HIDDEN, key_sets[0].astype(jnp.float32))
        key_sets[0] = own.astype(jnp.bfloat16)
    start, stop = doc_lanes(doc_ref, shape[0])
    order = row_order(rows, plan.rates, (held, LANES), 0)
    spots = jnp.concatenate([(order + head) & (rows - 1)] * heads, axis=0)
    for i in range(1, chunks):
        token = ((chunk ^ i) * heads + (head ^ lax.div(index, held))) * rows + spots
        at = plan.far_place(i)
        parts = [block_of(j)[at : at + plan.reach] for j in every]
        if held < plan.reach:
            parts = [x.astype(jnp.float32)[:held] for x in parts]
        kv = jnp.concatenate(parts, axis=0).astype(jnp.bfloat16)
        marked = (token >= start) & (token < stop)
        key_sets.append(kv * low + key_lanes(marked, lane, padding))
        value_sets.append(kv * high + low)
    return queries, jnp.concatenate(key_sets, axis=0), jnp.concatenate(value_sets, axis=0)


def forward(queries, keys, values):
    scores = dot(queries, keys, (1, 1))
    peak = jnp.max(scores, axis=1, keepdims=True)
    weights = jnp.exp(scores - peak).astype(jnp.bfloat16)
    return jnp.broadcast_to(peak, (queries.shape[0], LANES)), dot(weights, values, (1, 0))


def backward(queries, upstream, keys, values):
    probability = jnp.exp(dot(keys, queries, (1, 1)))
    shifted = (probability * dot(values, upstream, (1, 1))).astype(jnp.bfloat16)
    for_keys = dot(shifted, queries, (1, 0))
    for_values = dot(probability.astype(jnp.bfloat16), upstream, (1, 0))
    key_low = lane_of(for_keys.shape) < HEAD_DIM
    return dot(shifted, keys, (0, 0)), jnp.where(key_low, for_keys, for_values)


def merged(old_peak, old, peak, summed):
    new_peak = jnp.maximum(old_peak, peak)
    return new_peak, old * jnp.exp(old_peak - new_peak) + summed * jnp.exp(peak - new_peak)


def tiles(total, count, span):
    per_tile = max(1, QUERY_TILE // count)
    for start in range(0, total, span):
        for begin in range(start, start + span, per_tile):
            yield range(start, start + span), range(begin, min(begin + per_tile, start + span))


def pieces(x):
    first = x.astype(jnp.bfloat16).astype(jnp.float32)
    second = (x - first).astype(jnp.bfloat16).astype(jnp.float32)
    return first, second, x - first - second


def in_lanes(x, at):
    first, second, third = pieces(x)
    lane = lane_of(x.shape)
    value = jnp.where(lane == at, first, jnp.where(lane == at + 1, second, jnp.where(lane == at + 2, third, 0.0)))
    return value.astype(jnp.bfloat16)


def message_block(plan, refs, order, j):
    return refs[order.index(j & ~plan.bit)].at[1 if j & plan.bit else 0]


def ahead_kernel(plan, base, doc_ref, *refs):
    order = plan.group_order(base)
    x_refs, (qa, ka, va, ga, acc, top) = refs[: len(order)], refs[len(order) :]
    heads, rows = plan.heads, plan.rows
    chunk, head = my_place(heads)
    lane = lane_of((rows, LANES))
    spot = (row_order(rows, plan.rates, (rows, LANES), 0) + head) & (rows - 1)
    start, stop = doc_lanes(doc_ref, rows)
    low, high = lane_mask(rows, 1.0, 0.0), lane_mask(rows, 0.0, 1.0)
    low_scaled = lane_mask(rows, HEAD_DIM**-0.5, 0.0)
    for j in range(plan.group):
        token = (chunk * heads + (head ^ (base + j))) * rows + spot
        marked = (token >= start) & (token < stop)
        x = message_block(plan, x_refs, order, base + j)
        qg, kv = x[0:rows], x[rows : 2 * rows]
        qa[j] = qg * low_scaled + jnp.where(marked, 1.0, 0.0).astype(jnp.bfloat16)
        ka[j] = kv * low + key_lanes(marked, lane, None)
        va[j] = kv * high + low
        ga[j] = qg * high
    for level, (count, span) in enumerate(plan.near[:2]):
        for key_blocks, blocks in tiles(plan.group, count, span):
            peak, summed = forward(*(rows_of(r, b, count) for r, b in ((qa, blocks), (ka, key_blocks), (va, key_blocks))))
            if level > 0:
                peak, summed = merged(rows_of(top, blocks, count), rows_of(acc, blocks, count), peak, summed)
            set_rows(top, blocks, count, peak)
            set_rows(acc, blocks, count, summed)


def middle_kernel(plan, doc_ref, *refs):
    groups, refs = plan.heads // plan.group, list(refs)

    def take(count):
        taken = refs[:count]
        del refs[:count]
        return taken

    x_refs = take(len(plan.steps))
    qa, ka, va, ga, acc_in, top_in, qb, gb, output, dq_out, dkv_out, far_out = [take(groups) for _ in range(12)]
    acc, top, dq, dkv, far_sum = refs
    heads, rows, reach, size = plan.heads, plan.rows, plan.reach, plan.group
    every = range(heads)

    def block_of(j):
        return message_block(plan, x_refs, plan.order, j)

    def near_rows(kinds, key_blocks, blocks, count):
        return [rows_among(refs, key_blocks if is_key else blocks, count) for refs, is_key in kinds]

    for j in every:
        acc[j], top[j] = acc_in[j // size][j % size, 0:reach], top_in[j // size][j % size, 0:reach]

    def join(blocks, count, peak, summed):
        peak, summed = merged(rows_of(top, blocks, count), rows_of(acc, blocks, count), peak, summed)
        set_rows(top, blocks, count, peak)
        set_rows(acc, blocks, count, summed)

    for count, span in plan.near[2:]:
        for key_blocks, blocks in tiles(heads, count, span):
            join(blocks, count, *forward(*near_rows(((qa, 0), (ka, 1), (va, 1)), key_blocks, blocks, count)))
    for level, (_, held, _) in enumerate(plan.far):
        join(every, held, *forward(*far_operands(plan, level, doc_ref, qa, ka, va, block_of)))

    is_low = lane_of((rows, LANES)) < HEAD_DIM
    for j in every:
        g, b = divmod(j, size)
        summed = jnp.concatenate([acc[j], acc_in[g][b, reach:]], axis=0)
        peak = jnp.concatenate([top[j], top_in[g][b, reach:]], axis=0)
        total = jnp.where(is_low, summed, pltpu.roll(summed, HEAD_DIM, 1))
        normal = summed / total
        upstream = ga[g][b]
        delta = jnp.sum(normal * upstream.astype(jnp.float32), axis=1, keepdims=True)
        qb[g][b] = qa[g][b] + in_lanes(-(peak + jnp.log(total)), TOTAL_LANE)
        gb[g][b] = upstream + in_lanes(jnp.broadcast_to(-delta, (rows, LANES)), 0)
        output[g][b] = normal

    dq[...], dkv[...], far_sum[...] = jnp.zeros_like(dq), jnp.zeros_like(dkv), jnp.zeros_like(far_sum)
    for count, span in plan.near[2:]:
        for key_blocks, blocks in tiles(heads, count, span):
            for_queries, for_keys = backward(
                *near_rows(((qb, 0), (gb, 0), (ka, 1), (va, 1)), key_blocks, blocks, count)
            )
            add_rows(dq, blocks, count, for_queries)
            add_rows(dkv, key_blocks, count, for_keys)
    for level, (_, held, chunks) in enumerate(plan.far):
        queries, keys, values = far_operands(plan, level, doc_ref, qb, ka, va, block_of)
        for_queries, for_keys = backward(queries, rows_among(gb, every, held), keys, values)
        whole = heads * held
        add_rows(dq, every, held, for_queries)
        add_rows(dkv, every, held, for_keys[:whole])
        for i in range(1, chunks):
            add_rows(far_sum.at[i - 1], every, held, for_keys[i * whole : (i + 1) * whole])
    for j in every:
        g, b = divmod(j, size)
        dq_out[g][b], dkv_out[g][b] = dq[j], dkv[j]
        for i in range(plan.others):
            far_out[g][b, i * reach : (i + 1) * reach] = far_sum[i, j].astype(jnp.bfloat16)


def behind_kernel(plan, base, qb, ka, va, gb, output, dq_in, dkv_in, far_in, *refs):
    out_refs, (dq, dkv) = refs[:-2], refs[-2:]
    rows, every = plan.rows, range(plan.group)
    for level, (count, span) in enumerate(plan.near[:2]):
        for key_blocks, blocks in tiles(plan.group, count, span):
            for_queries, for_keys = backward(
                *(rows_of(r, b, count) for r, b in ((qb, blocks), (gb, blocks), (ka, key_blocks), (va, key_blocks)))
            )
            (add_rows if level else set_rows)(dq, blocks, count, for_queries)
            fresh = level == 0 and blocks.start == key_blocks.start
            (set_rows if fresh else add_rows)(dkv, key_blocks, count, for_keys)
    add_rows(dq, every, plan.reach, rows_of(dq_in, every, plan.reach))
    add_rows(dkv, every, plan.reach, rows_of(dkv_in, every, plan.reach))
    is_low = lane_of((rows, LANES)) < HEAD_DIM
    for j in every:
        out = message_block(plan, out_refs, plan.group_order(base), base + j)
        out[0:rows] = jnp.where(is_low, dq[j] * HEAD_DIM**-0.5, output[j]).astype(jnp.bfloat16)
        out[rows : 2 * rows] = dkv[j].astype(jnp.bfloat16)
        if plan.others:
            out[2 * rows :] = far_in[j]


def landed(x):
    return pltpu.VMEM(x.shape, x.dtype)


def call(kernel, out_shapes, args, scratch=(), flops=0, inputs=pltpu.VMEM, limit=VMEM_LIMIT):
    moved = sum(x.size * x.dtype.itemsize for x in (*args, *out_shapes))
    return pl.pallas_call(
        kernel,
        out_shape=out_shapes,
        in_specs=[pl.BlockSpec(memory_space=inputs)] * len(args),
        out_specs=[pl.BlockSpec(memory_space=pltpu.VMEM)] * len(out_shapes),
        scratch_shapes=scratch,
        compiler_params=pltpu.CompilerParams(vmem_limit_bytes=limit),
        cost_estimate=pl.CostEstimate(flops=flops, bytes_accessed=moved, transcendentals=0),
    )(*args)


def body(queries, keys, values, grad_out, doc_ids):
    rows, width = queries.shape
    shards, parts = lax.axis_size("seq"), lax.axis_size("head")
    devices = shards * parts
    plan = plan_of(rows, width, shards, parts)
    heads, steps, others = plan.heads, plan.steps, range(1, plan.others + 1)

    def swap(x, distance):
        return lax.ppermute(x, ("seq", "head"), [(d, d ^ distance) for d in range(devices)])

    def run(kernel, *rest, **more):
        return call(functools.partial(kernel, plan), *rest, **more)

    def array(*dims, dtype=jnp.bfloat16):
        return jax.ShapeDtypeStruct((*dims, LANES), dtype)

    blocks, far = array(len(steps), 2 * rows), array(len(steps), plan.reach)
    inputs = (queries, keys, values, grad_out)
    landing = [landed(array(len(steps) // 2, 4, rows)), pltpu.SemaphoreType.DMA((len(steps) // 2, 4))]

    def first_stage(send, same, cross):
        moved = [swap(cross[i - 1], i * heads ^ plan.bit) for i in others]
        moved = [swap(same[i - 1], i * heads) for i in others] + moved
        return [swap(send, plan.bit), *moved]

    send, cross = run(
        send_kernel, [blocks, far], inputs, landing, flops=1 << 26, inputs=pltpu.HBM, limit=PACK_LIMIT
    )
    keep, same = run(keep_kernel, [blocks, far], inputs, flops=1 << 26)
    arrived = first_stage(send, [same] * plan.others, [cross] * plan.others)
    message = array(2, plan.message)
    joined = run(join_kernel, [message] * len(steps), (keep, *arrived))
    chunk = [swap(x, step) if step else x for x, step in zip(joined, plan.order)]

    docs, bases, size, full = doc_ids.reshape(-1, LANES), range(0, heads, plan.group), plan.group, jnp.float32
    operand, total, prefix = array(size, rows), array(size, rows, dtype=full), array(size, plan.reach, dtype=full)
    ahead = [
        call(
            functools.partial(ahead_kernel, plan, base),
            [operand] * 4 + [total] * 2,
            (docs, *(chunk[plan.order.index(m)] for m in plan.group_order(base))),
            flops=1 << 28,
        )
        for base in bases
    ]
    qa, ka, va, ga, acc, top = zip(*ahead)
    scratch = [array(heads, plan.reach, dtype=full)] * 4 + [array(max(1, plan.others), heads, plan.reach, dtype=full)]
    far_part = array(size, max(1, plan.others) * plan.reach)
    middle = run(
        middle_kernel,
        [x for x in (operand, operand, total, prefix, prefix, far_part) for _ in bases],
        (docs, *chunk, *qa, *ka, *va, *ga, *acc, *top),
        [landed(x) for x in scratch],
        flops=1 << 28,
    )
    state = [middle[n :: len(bases)] for n in range(len(bases))]
    grads = {}
    for base, ka_part, va_part, (qb, gb, *others_in) in zip(bases, ka, va, state):
        names = plan.group_order(base)
        parts_out = call(
            functools.partial(behind_kernel, plan, base),
            [message] * len(names),
            (qb, ka_part, va_part, gb, *others_in),
            [landed(total)] * 2,
            flops=1 << 28,
        )
        grads.update(zip(names, parts_out))
    back = [swap(grads[step], step) if step else grads[step] for step in plan.order]
    sent = run(part_kernel, [blocks] + [far] * (2 * plan.others), back)
    returned = first_stage(sent[0], sent[1 : 1 + plan.others], sent[1 + plan.others :])
    result = [jax.ShapeDtypeStruct((rows, width), jnp.bfloat16)] * 4
    return tuple(run(unpack_kernel, result, (*back, *returned), flops=1 << 27))


def solution(mesh):
    split = P(("seq", "head"), None)
    return jax.shard_map(
        body, mesh=mesh, in_specs=(split,) * 4 + (P(),), out_specs=(split,) * 4, check_vma=False
    )
```

```python
import dataclasses
import functools

import jax
import jax.numpy as jnp
from jax import lax
from jax.experimental import pallas as pl
from jax.experimental.pallas import tpu as pltpu
from jax.sharding import PartitionSpec as P

HEAD_DIM = 64
LANES = 2 * HEAD_DIM
HIDDEN = -131072.0
DOC_LANE, TOTAL_LANE, QUERY_PAD, KEY_PAD = HEAD_DIM, HEAD_DIM + 3, HEAD_DIM + 6, HEAD_DIM + 7
QUERY_TILE = 256
FAR_ROWS = 8
COPY_PARTS = 4
PACK_LIMIT = 56 * 1024 * 1024
VMEM_LIMIT = 14 * 1024 * 1024


def dot(a, b, contract):
    return lax.dot_general(a, b, ((contract[:1], contract[1:]), ((), ())), preferred_element_type=jnp.float32)


def row_order(rows, rates, shape, axis):
    row = lax.broadcasted_iota(jnp.int32, shape, axis)
    order = row * rates[-1]
    for rate, above in zip(rates[-2::-1], rates[:0:-1]):
        between, fresh = above // rate - 1, row - rows // above
        if between > 0:
            group = fresh if between == 1 else lax.div(fresh, between)
            order = jnp.where(fresh >= 0, group * above + (fresh - group * between + 1) * rate, order)
    return order


def lane_of(shape):
    return lax.broadcasted_iota(jnp.int32, shape, 1)


def halves_swapped(x):
    return jnp.concatenate([x[:, HEAD_DIM:], x[:, :HEAD_DIM]], axis=1)


def lane_mask(rows, at_low, at_high):
    return jnp.where(lane_of((rows, LANES)) < HEAD_DIM, at_low, at_high).astype(jnp.bfloat16)


def pack_kernel(rates, q_hbm, k_hbm, v_hbm, g_hbm, out_hbm, q_ref, k_ref, v_ref, g_ref, out_ref, arrived, left):
    rows, width = q_ref.shape
    copies, outgoing = [], []
    for part in range(COPY_PARTS):
        cols = pl.ds(part * (width // COPY_PARTS), width // COPY_PARTS)
        held = ((q_hbm, q_ref), (k_hbm, k_ref), (v_hbm, v_ref), (g_hbm, g_ref))
        copies.append(
            [pltpu.make_async_copy(a.at[:, cols], b.at[:, cols], arrived.at[part, i]) for i, (a, b) in enumerate(held)]
        )
    for part in copies:
        for copy in part:
            copy.start()
    order = row_order(rows, rates, (rows, rows), 0)
    lane = lane_of((rows, rows))
    low, high = lane_mask(rows, 1.0, 0.0), lane_mask(rows, 0.0, 1.0)
    for tile in range(width // LANES):
        cols = slice(tile * LANES, (tile + 1) * LANES)
        part, inside = divmod(tile * LANES, width // COPY_PARTS)
        if inside == 0:
            for copy in copies[part]:
                copy.wait()
        pairs = ((q_ref[:, cols], g_ref[:, cols]), (k_ref[:, cols], v_ref[:, cols]))
        even = [first * low + halves_swapped(second) * high for first, second in pairs]
        odd = [halves_swapped(first) * low + second * high for first, second in pairs]
        for side, sources in enumerate((even, odd)):
            pick = jnp.where(order == ((lane - (2 * tile + side)) & (rows - 1)), 1.0, 0.0).astype(jnp.bfloat16)
            moved = dot(pick, jnp.concatenate(sources, axis=1), (1, 0)).astype(jnp.bfloat16)
            out_ref[2 * tile + side, 0] = moved[:, :LANES]
            out_ref[2 * tile + side, 1] = moved[:, LANES:]
        if inside + LANES == width // COPY_PARTS:
            done = pl.ds(part * (width // HEAD_DIM // COPY_PARTS), width // HEAD_DIM // COPY_PARTS)
            outgoing.append(pltpu.make_async_copy(out_ref.at[done], out_hbm.at[done], left.at[part]))
            outgoing[-1].start()
    for copy in outgoing:
        copy.wait()


def unpack_kernel(rates, in_ref, *refs):
    (out_hbm, dq_hbm, dk_hbm, dv_hbm), (out_ref, dq_ref, dk_ref, dv_ref, left) = refs[:4], refs[4:]
    rows, width = out_ref.shape
    outgoing = []
    order = row_order(rows, rates, (rows, rows), 1)
    token = lax.broadcasted_iota(jnp.int32, (rows, rows), 0)
    low, high = lane_mask(rows, 1.0, 0.0), lane_mask(rows, 0.0, 1.0)
    for tile in range(width // LANES):
        cols = slice(tile * LANES, (tile + 1) * LANES)
        picks, sources = [], []
        for side in range(2):
            head = 2 * tile + side
            picks.append(jnp.where(((order + head) & (rows - 1)) == token, 1.0, 0.0).astype(jnp.bfloat16))
            columns = []
            for kind in range(2):
                x = in_ref[head, kind]
                y = halves_swapped(x)
                columns += [y * high, x * high] if side else [x * low, y * low]
            sources.append(jnp.concatenate(columns, axis=1))
        moved = dot(jnp.concatenate(picks, axis=1), jnp.concatenate(sources, axis=0), (1, 0)).astype(jnp.bfloat16)
        for i, ref in enumerate((dq_ref, out_ref, dk_ref, dv_ref)):
            ref[:, cols] = moved[:, i * LANES : (i + 1) * LANES]
        part, inside = divmod((tile + 1) * LANES, width // COPY_PARTS)
        if inside == 0:
            done = pl.ds((part - 1) * (width // COPY_PARTS), width // COPY_PARTS)
            held = ((out_ref, out_hbm), (dq_ref, dq_hbm), (dk_ref, dk_hbm), (dv_ref, dv_hbm))
            for i, (a, b) in enumerate(held):
                outgoing.append(pltpu.make_async_copy(a.at[:, done], b.at[:, done], left.at[part - 1, i]))
                outgoing[-1].start()
    for copy in outgoing:
        copy.wait()


@dataclasses.dataclass(frozen=True)
class Plan:
    heads: int
    rows: int
    rates: tuple
    near: tuple
    far: tuple

    @property
    def late(self):
        return self.near[2:], max([count for count, _ in self.near[2:]] + [held for _, held, _ in self.far])


def plan_of(rows, width, shards, parts):
    heads, rates = width // HEAD_DIM, (1, 2, 8, shards)
    near, far = [], []
    for rate in rates:
        span = rows * parts * rate
        if span <= rows * heads:
            near.append((rows // rate, span // rows))
        else:
            far.append((rows // rate, max(rows // rate, FAR_ROWS), span // (rows * heads)))
    return Plan(heads, rows, rates, tuple(near), tuple(far))


def my_place(heads):
    index = lax.axis_index("seq") * lax.axis_size("head") + lax.axis_index("head")
    return lax.div(index, heads), index & (heads - 1)


def rows_of(ref, blocks, count):
    if count == ref.shape[1]:
        return ref[blocks.start : blocks.stop].reshape(len(blocks) * count, LANES)
    if ref.dtype == jnp.bfloat16 and count % 16:
        held = -(-count // 16) * 16
        parts = [ref[j, 0:held].astype(jnp.float32)[0:count] for j in blocks]
        return jnp.concatenate(parts, axis=0).astype(jnp.bfloat16)
    return jnp.concatenate([ref[j, 0:count] for j in blocks], axis=0)


def set_rows(ref, blocks, count, value):
    for i, j in enumerate(blocks):
        ref[j, 0:count] = value[i * count : (i + 1) * count]


def add_rows(ref, blocks, count, value):
    set_rows(ref, blocks, count, rows_of(ref, blocks, count) + value)


def doc_lanes(doc_ref, rows):
    docs = doc_ref[...]
    first, second = [jnp.sum(jnp.where(docs < d, 1, 0)) for d in (1, 2)]
    lane, last = lane_of((rows, LANES)), jnp.iinfo(jnp.int32).max
    start, stop = jnp.full((rows, LANES), last, jnp.int32), jnp.full((rows, LANES), 0, jnp.int32)
    for at, lo, hi in ((0, 0, first), (1, first, second), (2, second, last), (KEY_PAD - DOC_LANE, 0, last)):
        start = jnp.where(lane == DOC_LANE + at, lo, start)
        stop = jnp.where(lane == DOC_LANE + at, hi, stop)
    return start, stop


def key_lanes(marked, lane, padding):
    outside = jnp.where((lane >= TOTAL_LANE) & (lane <= QUERY_PAD), 1.0, 0.0)
    outside = jnp.where((lane >= DOC_LANE) & (lane < TOTAL_LANE), HIDDEN, outside)
    value = jnp.where(marked, 0.0, outside)
    if padding is not None:
        value = jnp.where((lane == KEY_PAD) & padding, HIDDEN, value)
    return value.astype(jnp.bfloat16)


def far_operands(plan, level, doc_ref, qa, ka, va, far_ref):
    count, held, chunks = plan.far[level]
    heads, rows = plan.heads, plan.rows
    chunk, head = my_place(heads)
    every, shape = range(heads), (heads * held, LANES)
    lane, index = lane_of(shape), lax.broadcasted_iota(jnp.int32, shape, 0)
    low, high = lane_mask(shape[0], 1.0, 0.0), lane_mask(shape[0], 0.0, 1.0)
    padding = None if count == held else (index & (held - 1)) >= count
    queries = rows_of(qa, every, held)
    key_sets, value_sets = [rows_of(ka, every, held)], [rows_of(va, every, held)]
    if padding is not None:
        queries = jnp.where((lane == QUERY_PAD) & padding, HIDDEN, queries.astype(jnp.float32)).astype(jnp.bfloat16)
        own = jnp.where((lane == KEY_PAD) & padding, HIDDEN, key_sets[0].astype(jnp.float32))
        key_sets[0] = own.astype(jnp.bfloat16)
    start, stop = doc_lanes(doc_ref, shape[0])
    order = row_order(rows, plan.rates, (held, LANES), 0)
    spots = jnp.concatenate([(order + head) & (rows - 1)] * heads, axis=0)
    for i in range(1, chunks):
        token = ((chunk ^ i) * heads + lax.div(index, held)) * rows + spots
        marked = (token >= start) & (token < stop)
        key_sets.append(far_ref[i - 1] * low + key_lanes(marked, lane, padding))
        value_sets.append(far_ref[i - 1] * high + low)
    return queries, jnp.concatenate(key_sets, axis=0), jnp.concatenate(value_sets, axis=0)


def forward(queries, keys, values):
    scores = dot(queries, keys, (1, 1))
    peak = jnp.max(scores, axis=1, keepdims=True)
    weights = jnp.exp(scores - peak).astype(jnp.bfloat16)
    return jnp.broadcast_to(peak, (queries.shape[0], LANES)), dot(weights, values, (1, 0))


def backward(queries, upstream, keys, values):
    probability = jnp.exp(dot(keys, queries, (1, 1)))
    shifted = (probability * dot(values, upstream, (1, 1))).astype(jnp.bfloat16)
    for_keys = dot(shifted, queries, (1, 0))
    for_values = dot(probability.astype(jnp.bfloat16), upstream, (1, 0))
    key_low = lane_of(for_keys.shape) < HEAD_DIM
    return dot(shifted, keys, (0, 0)), jnp.where(key_low, for_keys, for_values)


def merged(old_peak, old, peak, summed):
    new_peak = jnp.maximum(old_peak, peak)
    return new_peak, old * jnp.exp(old_peak - new_peak) + summed * jnp.exp(peak - new_peak)


def tiles(plan, count, span):
    per_tile = max(1, QUERY_TILE // count)
    for start in range(0, plan.heads, span):
        for begin in range(start, start + span, per_tile):
            yield range(start, start + span), range(begin, min(begin + per_tile, start + span))


def near_kernel(plan, doc_ref, x_ref, qa, ka, va, ga, acc, top):
    heads, rows = plan.heads, plan.rows
    chunk, head = my_place(heads)
    lane = lane_of((rows, LANES))
    spot = (row_order(rows, plan.rates, (rows, LANES), 0) + head) & (rows - 1)
    start, stop = doc_lanes(doc_ref, rows)
    low, high = lane_mask(rows, 1.0, 0.0), lane_mask(rows, 0.0, 1.0)
    low_scaled = lane_mask(rows, HEAD_DIM**-0.5, 0.0)
    for j in range(heads):
        token = (chunk * heads + j) * rows + spot
        marked = (token >= start) & (token < stop)
        qg, kv = x_ref[j, 0], x_ref[j, 1]
        qa[j] = qg * low_scaled + jnp.where(marked, 1.0, 0.0).astype(jnp.bfloat16)
        ka[j] = kv * low + key_lanes(marked, lane, None)
        va[j] = kv * high + low
        ga[j] = qg * high
    for level, (count, span) in enumerate(plan.near):
        for key_blocks, blocks in tiles(plan, count, span):
            peak, summed = forward(*(rows_of(r, b, count) for r, b in ((qa, blocks), (ka, key_blocks), (va, key_blocks))))
            if level > 0:
                peak, summed = merged(rows_of(top, blocks, count), rows_of(acc, blocks, count), peak, summed)
            set_rows(top, blocks, count, peak)
            set_rows(acc, blocks, count, summed)


def pieces(x):
    first = x.astype(jnp.bfloat16).astype(jnp.float32)
    second = (x - first).astype(jnp.bfloat16).astype(jnp.float32)
    return first, second, x - first - second


def far_kernel(plan, doc_ref, qa, ka, va, ga, acc_in, top_in, *refs):
    levels = len(plan.far)
    far_in, refs = refs[:levels], refs[levels:]
    (qb, gb, output), refs = refs[:3], refs[3:]
    far_dq, far_dkv, far_out, (acc, top) = refs[:levels], refs[levels : 2 * levels], refs[2 * levels : -2], refs[-2:]
    heads, rows = plan.heads, plan.rows
    every = range(heads)
    _, reach = plan.late
    for j in every:
        acc[j], top[j] = acc_in[j, 0:reach], top_in[j, 0:reach]
    for level, (_, held, _) in enumerate(plan.far):
        peak, summed = forward(*far_operands(plan, level, doc_ref, qa, ka, va, far_in[level]))
        peak, summed = merged(rows_of(top, every, held), rows_of(acc, every, held), peak, summed)
        set_rows(top, every, held, peak)
        set_rows(acc, every, held, summed)

    lane = lane_of((rows, LANES))
    total, peak, dots = jnp.ones((rows, LANES), jnp.float32), *[jnp.zeros((rows, LANES), jnp.float32)] * 2
    sums = []
    for j in every:
        sums.append(jnp.concatenate([acc[j], acc_in[j, reach:]], axis=0))
        dot_j = jnp.sum(sums[j] * ga[j].astype(jnp.float32), axis=1, keepdims=True)
        total = jnp.where(lane == j, sums[j], total)
        peak = jnp.where(lane == j, jnp.concatenate([top[j], top_in[j, reach:]], axis=0), peak)
        dots = jnp.where(lane == j, dot_j, dots)
    inverse = 1.0 / total
    held_pieces = [*pieces(-(peak + jnp.log(total))), *pieces(-(dots * inverse))]
    moved = held_pieces[0]
    for i, piece in enumerate(held_pieces[1:]):
        moved = moved + pltpu.roll(piece, (i + 1) * heads, 1)
    moved = moved.astype(jnp.bfloat16)
    column = lane_of((LANES, 2 * LANES))
    source = lax.broadcasted_iota(jnp.int32, column.shape, 0)
    wanted = jnp.full(column.shape, -LANES, jnp.int32)
    for i in range(3):
        wanted = jnp.where(column == TOTAL_LANE + i, i * heads, wanted)
        wanted = jnp.where(column == LANES + i, (3 + i) * heads, wanted)
    wanted = source - wanted
    for j in every:
        place_j = jnp.where(wanted == j, 1.0, 0.0).astype(jnp.bfloat16)
        added = dot(moved, place_j, (1, 0)).astype(jnp.bfloat16)
        qb[j] = qa[j] + added[:, :LANES]
        gb[j] = ga[j] + added[:, LANES:]
        output[j] = sums[j] * inverse[:, j : j + 1]

    for level, (_, held, chunks) in enumerate(plan.far):
        queries, keys, values = far_operands(plan, level, doc_ref, qb, ka, va, far_in[level])
        for_queries, for_keys = backward(queries, rows_of(gb, every, held), keys, values)
        size = heads * held
        far_dq[level][...] = for_queries
        far_dkv[level][...] = for_keys[:size]
        for i in range(1, chunks):
            far_out[level][i - 1] = for_keys[i * size : (i + 1) * size].astype(jnp.bfloat16)


def local_kernel(plan, qb, ka, va, gb, dq, dkv):
    for level, (count, span) in enumerate(plan.near[:2]):
        for key_blocks, blocks in tiles(plan, count, span):
            for_queries, for_keys = backward(
                *(rows_of(r, b, count) for r, b in ((qb, blocks), (gb, blocks), (ka, key_blocks), (va, key_blocks)))
            )
            (add_rows if level else set_rows)(dq, blocks, count, for_queries)
            fresh = level == 0 and blocks.start == key_blocks.start
            (set_rows if fresh else add_rows)(dkv, key_blocks, count, for_keys)


def last_kernel(plan, qb, ka, va, gb, output, dq_in, dkv_in, *refs):
    levels = len(plan.far)
    far_dq, far_dkv, far_back = refs[:levels], refs[levels : 2 * levels], refs[2 * levels : 3 * levels]
    out_ref, dq, dkv = refs[3 * levels :]
    heads, rows = plan.heads, plan.rows
    every, (near, reach) = range(heads), plan.late
    for j in every:
        dq[j], dkv[j] = dq_in[j, 0:reach], dkv_in[j, 0:reach]
    for count, span in near:
        for key_blocks, blocks in tiles(plan, count, span):
            for_queries, for_keys = backward(
                *(rows_of(r, b, count) for r, b in ((qb, blocks), (gb, blocks), (ka, key_blocks), (va, key_blocks)))
            )
            add_rows(dq, blocks, count, for_queries)
            add_rows(dkv, key_blocks, count, for_keys)
    for level, (_, held, chunks) in enumerate(plan.far):
        add_rows(dq, every, held, far_dq[level][...])
        partial = far_dkv[level][...]
        for i in range(1, chunks):
            partial = partial + far_back[level][i - 1].astype(jnp.float32)
        add_rows(dkv, every, held, partial)
    low = lane_of((rows, LANES)) < HEAD_DIM
    for j in every:
        for_queries = jnp.concatenate([dq[j], dq_in[j, reach:]], axis=0)
        out_ref[j, 0] = jnp.where(low, for_queries * HEAD_DIM**-0.5, output[j]).astype(jnp.bfloat16)
        out_ref[j, 1] = jnp.concatenate([dkv[j], dkv_in[j, reach:]], axis=0).astype(jnp.bfloat16)


def landed(x):
    return pltpu.VMEM(x.shape, x.dtype)


def call(kernel, out_shapes, args, scratch=(), flops=0, inputs=pltpu.VMEM, outputs=pltpu.VMEM, limit=VMEM_LIMIT):
    moved = sum(x.size * x.dtype.itemsize for x in (*args, *out_shapes))
    return pl.pallas_call(
        kernel,
        out_shape=out_shapes,
        in_specs=[pl.BlockSpec(memory_space=inputs)] * len(args),
        out_specs=[pl.BlockSpec(memory_space=outputs)] * len(out_shapes),
        scratch_shapes=scratch,
        compiler_params=pltpu.CompilerParams(vmem_limit_bytes=limit),
        cost_estimate=pl.CostEstimate(flops=flops, bytes_accessed=moved, transcendentals=0),
    )(*args)


def body(queries, keys, values, grad_out, doc_ids):
    rows, width = queries.shape
    shards, parts = lax.axis_size("seq"), lax.axis_size("head")
    devices, axes = shards * parts, ("seq", "head")
    plan = plan_of(rows, width, shards, parts)
    heads, _, (_, reach) = plan.heads, plan.far, plan.late
    groups = [[c * heads + h for h in range(heads)] for c in range(devices // heads)]

    def exchange(x):
        return lax.all_to_all(x, axes, 0, 0, axis_index_groups=groups, tiled=True)

    def from_chunk(x, i):
        return lax.ppermute(x, axes, [(d, d ^ (i * heads)) for d in range(devices)])

    def run(kernel, *rest, **more):
        return call(functools.partial(kernel, plan), *rest, **more)

    shape, low, full = jax.ShapeDtypeStruct, jnp.bfloat16, jnp.float32
    packed = shape((heads, 2, rows, LANES), low)
    operand, total = shape((heads, rows, LANES), low), shape((heads, rows, LANES), full)
    prefix = shape((heads, reach, LANES), full)
    own_far = [shape((heads * held, LANES), full) for _, held, _ in plan.far]
    docs = doc_ids.reshape(-1, LANES)

    inputs = (queries, keys, values, grad_out)
    semaphores = pltpu.SemaphoreType.DMA((COPY_PARTS, len(inputs)))
    landing = [landed(x) for x in (*inputs, packed)] + [semaphores, pltpu.SemaphoreType.DMA((COPY_PARTS,))]
    mine = call(
        functools.partial(pack_kernel, plan.rates), [packed], inputs, landing, flops=1 << 27, inputs=pltpu.HBM, outputs=pltpu.HBM, limit=PACK_LIMIT
    )[0]
    chunk = exchange(mine)
    gathered = []
    for _, held, chunks in plan.far:
        picked = chunk[:, 1, :held].reshape(heads * held, LANES)
        gathered.append(jnp.stack([from_chunk(picked, i) for i in range(1, chunks)]))
    qa, ka, va, ga, acc, top = run(near_kernel, [operand] * 4 + [total] * 2, (docs, chunk), flops=1 << 30)
    sent = [shape(x.shape, x.dtype) for x in gathered]
    qb, gb, output, *rest = run(
        far_kernel,
        [operand] * 2 + [total] + own_far * 2 + sent,
        (docs, qa, ka, va, ga, acc, top, *gathered),
        [landed(prefix)] * 2,
        flops=1 << 28,
    )
    owned, partials = rest[: 2 * len(plan.far)], rest[2 * len(plan.far) :]
    returned = [jnp.stack([from_chunk(x[i], i + 1) for i in range(x.shape[0])]) for x in partials]
    dq, dkv = run(local_kernel, [total] * 2, (qb, ka, va, gb), flops=1 << 30)
    grads = run(
        last_kernel, [packed], (qb, ka, va, gb, output, dq, dkv, *owned, *returned), [landed(prefix)] * 2, flops=1 << 28
    )[0]
    result = [shape((rows, width), low)] * 4
    leaving = [landed(x) for x in result] + [semaphores]
    unpack = functools.partial(unpack_kernel, plan.rates)
    return tuple(call(unpack, result, (exchange(grads),), leaving, flops=1 << 27, outputs=pltpu.HBM))


def solution(mesh):
    split = P(("seq", "head"), None)
    return jax.shard_map(
        body, mesh=mesh, in_specs=(split,) * 4 + (P(),), out_specs=(split,) * 4, check_vma=False
    )
```

```python
import dataclasses
import functools

import jax
import jax.numpy as jnp
from jax import lax
from jax.experimental import pallas as pl
from jax.experimental.pallas import tpu as pltpu
from jax.sharding import PartitionSpec as P

HEAD_DIM = 64
LANES = 2 * HEAD_DIM
HIDDEN = -131072.0
DOC_LANE, TOTAL_LANE, QUERY_PAD, KEY_PAD = HEAD_DIM, HEAD_DIM + 3, HEAD_DIM + 6, HEAD_DIM + 7
QUERY_TILE = 256
FAR_ROWS = 8
COPY_PARTS = 2
PACK_LIMIT = 56 * 1024 * 1024
VMEM_LIMIT = 14 * 1024 * 1024


def dot(a, b, contract):
    return lax.dot_general(a, b, ((contract[:1], contract[1:]), ((), ())), preferred_element_type=jnp.float32)


def row_order(rows, rates, shape, axis):
    row = lax.broadcasted_iota(jnp.int32, shape, axis)
    order = row * rates[-1]
    for rate, above in zip(rates[-2::-1], rates[:0:-1]):
        between, fresh = above // rate - 1, row - rows // above
        if between > 0:
            group = fresh if between == 1 else lax.div(fresh, between)
            order = jnp.where(fresh >= 0, group * above + (fresh - group * between + 1) * rate, order)
    return order


def lane_of(shape):
    return lax.broadcasted_iota(jnp.int32, shape, 1)


def halves_swapped(x):
    return jnp.concatenate([x[:, HEAD_DIM:], x[:, :HEAD_DIM]], axis=1)


def lane_mask(rows, at_low, at_high):
    return jnp.where(lane_of((rows, LANES)) < HEAD_DIM, at_low, at_high).astype(jnp.bfloat16)


def pack_kernel(rates, q_hbm, k_hbm, v_hbm, g_hbm, out_hbm, q_ref, k_ref, v_ref, g_ref, out_ref, arrived, left):
    rows, width = q_ref.shape
    heads = width // HEAD_DIM
    held = ((k_hbm, k_ref), (v_hbm, v_ref), (q_hbm, q_ref), (g_hbm, g_ref))
    copies = [pltpu.make_async_copy(a, b, arrived.at[i]) for i, (a, b) in enumerate(held)]
    for copy in copies:
        copy.start()
    order = row_order(rows, rates, (rows, rows), 0)
    lane = lane_of((rows, rows))
    low, high = lane_mask(rows, 1.0, 0.0), lane_mask(rows, 0.0, 1.0)
    outgoing = []
    for kind, first_ref, second_ref, waits in ((1, k_ref, v_ref, copies[:2]), (0, q_ref, g_ref, copies[2:])):
        for copy in waits:
            copy.wait()
        for tile in range(width // LANES):
            cols = slice(tile * LANES, (tile + 1) * LANES)
            first, second = first_ref[:, cols], second_ref[:, cols]
            even = first * low + halves_swapped(second) * high
            odd = halves_swapped(first) * low + second * high
            for side, source in enumerate((even, odd)):
                pick = jnp.where(order == ((lane - (2 * tile + side)) & (rows - 1)), 1.0, 0.0).astype(jnp.bfloat16)
                out_ref[2 * tile + side, kind] = dot(pick, source, (1, 0)).astype(jnp.bfloat16)
            if (2 * tile + 2) % (heads // COPY_PARTS) == 0:
                done = pl.ds(2 * tile + 2 - heads // COPY_PARTS, heads // COPY_PARTS)
                ready = left.at[kind, (2 * tile + 1) // (heads // COPY_PARTS)]
                outgoing.append(pltpu.make_async_copy(out_ref.at[done, kind], out_hbm.at[done, kind], ready))
                outgoing[-1].start()
    for copy in outgoing:
        copy.wait()


def unpack_kernel(rates, in_ref, *refs):
    (out_hbm, dq_hbm, dk_hbm, dv_hbm), (out_ref, dq_ref, dk_ref, dv_ref, left) = refs[:4], refs[4:]
    rows, width = out_ref.shape
    outgoing = []
    order = row_order(rows, rates, (rows, rows), 1)
    token = lax.broadcasted_iota(jnp.int32, (rows, rows), 0)
    low, high = lane_mask(rows, 1.0, 0.0), lane_mask(rows, 0.0, 1.0)
    for tile in range(width // LANES):
        cols = slice(tile * LANES, (tile + 1) * LANES)
        picks, sources = [], []
        for side in range(2):
            head = 2 * tile + side
            picks.append(jnp.where(((order + head) & (rows - 1)) == token, 1.0, 0.0).astype(jnp.bfloat16))
            columns = []
            for kind in range(2):
                x = in_ref[head, kind]
                y = halves_swapped(x)
                columns += [y * high, x * high] if side else [x * low, y * low]
            sources.append(jnp.concatenate(columns, axis=1))
        moved = dot(jnp.concatenate(picks, axis=1), jnp.concatenate(sources, axis=0), (1, 0)).astype(jnp.bfloat16)
        for i, ref in enumerate((dq_ref, out_ref, dk_ref, dv_ref)):
            ref[:, cols] = moved[:, i * LANES : (i + 1) * LANES]
        part, inside = divmod((tile + 1) * LANES, width // COPY_PARTS)
        if inside == 0:
            done = pl.ds((part - 1) * (width // COPY_PARTS), width // COPY_PARTS)
            held = ((out_ref, out_hbm), (dq_ref, dq_hbm), (dk_ref, dk_hbm), (dv_ref, dv_hbm))
            for i, (a, b) in enumerate(held):
                outgoing.append(pltpu.make_async_copy(a.at[:, done], b.at[:, done], left.at[part - 1, i]))
                outgoing[-1].start()
    for copy in outgoing:
        copy.wait()


@dataclasses.dataclass(frozen=True)
class Plan:
    heads: int
    rows: int
    rates: tuple
    near: tuple
    far: tuple

    @property
    def late(self):
        return self.near[2:], max([count for count, _ in self.near[2:]] + [held for _, held, _ in self.far])


def plan_of(rows, width, shards, parts):
    heads, rates = width // HEAD_DIM, (1, 2, 8, shards)
    near, far = [], []
    for rate in rates:
        span = rows * parts * rate
        if span <= rows * heads:
            near.append((rows // rate, span // rows))
        else:
            far.append((rows // rate, max(rows // rate, FAR_ROWS), span // (rows * heads)))
    return Plan(heads, rows, rates, tuple(near), tuple(far))


def my_place(heads):
    index = lax.axis_index("seq") * lax.axis_size("head") + lax.axis_index("head")
    return lax.div(index, heads), index & (heads - 1)


def rows_of(ref, blocks, count):
    if count == ref.shape[1]:
        return ref[blocks.start : blocks.stop].reshape(len(blocks) * count, LANES)
    if ref.dtype == jnp.bfloat16 and count % 16:
        held = -(-count // 16) * 16
        parts = [ref[j, 0:held].astype(jnp.float32)[0:count] for j in blocks]
        return jnp.concatenate(parts, axis=0).astype(jnp.bfloat16)
    return jnp.concatenate([ref[j, 0:count] for j in blocks], axis=0)


def set_rows(ref, blocks, count, value):
    for i, j in enumerate(blocks):
        ref[j, 0:count] = value[i * count : (i + 1) * count]


def add_rows(ref, blocks, count, value):
    set_rows(ref, blocks, count, rows_of(ref, blocks, count) + value)


def doc_lanes(doc_ref, rows):
    docs = doc_ref[...]
    first, second = [jnp.sum(jnp.where(docs < d, 1, 0)) for d in (1, 2)]
    lane, last = lane_of((rows, LANES)), jnp.iinfo(jnp.int32).max
    start, stop = jnp.full((rows, LANES), last, jnp.int32), jnp.full((rows, LANES), 0, jnp.int32)
    for at, lo, hi in ((0, 0, first), (1, first, second), (2, second, last), (KEY_PAD - DOC_LANE, 0, last)):
        start = jnp.where(lane == DOC_LANE + at, lo, start)
        stop = jnp.where(lane == DOC_LANE + at, hi, stop)
    return start, stop


def key_lanes(marked, lane, padding):
    outside = jnp.where((lane >= TOTAL_LANE) & (lane <= QUERY_PAD), 1.0, 0.0)
    outside = jnp.where((lane >= DOC_LANE) & (lane < TOTAL_LANE), HIDDEN, outside)
    value = jnp.where(marked, 0.0, outside)
    if padding is not None:
        value = jnp.where((lane == KEY_PAD) & padding, HIDDEN, value)
    return value.astype(jnp.bfloat16)


def far_operands(plan, level, doc_ref, qa, ka, va, far_ref):
    count, held, chunks = plan.far[level]
    heads, rows = plan.heads, plan.rows
    chunk, head = my_place(heads)
    every, shape = range(heads), (heads * held, LANES)
    lane, index = lane_of(shape), lax.broadcasted_iota(jnp.int32, shape, 0)
    low, high = lane_mask(shape[0], 1.0, 0.0), lane_mask(shape[0], 0.0, 1.0)
    padding = None if count == held else (index & (held - 1)) >= count
    queries = rows_of(qa, every, held)
    key_sets, value_sets = [rows_of(ka, every, held)], [rows_of(va, every, held)]
    if padding is not None:
        queries = jnp.where((lane == QUERY_PAD) & padding, HIDDEN, queries.astype(jnp.float32)).astype(jnp.bfloat16)
        own = jnp.where((lane == KEY_PAD) & padding, HIDDEN, key_sets[0].astype(jnp.float32))
        key_sets[0] = own.astype(jnp.bfloat16)
    start, stop = doc_lanes(doc_ref, shape[0])
    order = row_order(rows, plan.rates, (held, LANES), 0)
    spots = jnp.concatenate([(order + head) & (rows - 1)] * heads, axis=0)
    for i in range(1, chunks):
        token = ((chunk ^ i) * heads + lax.div(index, held)) * rows + spots
        marked = (token >= start) & (token < stop)
        key_sets.append(far_ref[i - 1] * low + key_lanes(marked, lane, padding))
        value_sets.append(far_ref[i - 1] * high + low)
    return queries, jnp.concatenate(key_sets, axis=0), jnp.concatenate(value_sets, axis=0)


def forward(queries, keys, values):
    scores = dot(queries, keys, (1, 1))
    peak = jnp.max(scores, axis=1, keepdims=True)
    weights = jnp.exp(scores - peak).astype(jnp.bfloat16)
    return jnp.broadcast_to(peak, (queries.shape[0], LANES)), dot(weights, values, (1, 0))


def backward(queries, upstream, keys, values):
    probability = jnp.exp(dot(keys, queries, (1, 1)))
    shifted = (probability * dot(values, upstream, (1, 1))).astype(jnp.bfloat16)
    for_keys = dot(shifted, queries, (1, 0))
    for_values = dot(probability.astype(jnp.bfloat16), upstream, (1, 0))
    key_low = lane_of(for_keys.shape) < HEAD_DIM
    for_queries = dot(keys.T[:HEAD_DIM], shifted, (1, 0)).T
    for_queries = jnp.concatenate([for_queries, jnp.zeros_like(for_queries)], axis=1)
    return for_queries, jnp.where(key_low, for_keys, for_values)


def merged(old_peak, old, peak, summed):
    new_peak = jnp.maximum(old_peak, peak)
    return new_peak, old * jnp.exp(old_peak - new_peak) + summed * jnp.exp(peak - new_peak)


def tiles(plan, count, span):
    per_tile = max(1, QUERY_TILE // count)
    for start in range(0, plan.heads, span):
        for begin in range(start, start + span, per_tile):
            yield range(start, start + span), range(begin, min(begin + per_tile, start + span))


def near_kernel(plan, doc_ref, x_ref, qa, ka, va, ga, acc, top):
    heads, rows = plan.heads, plan.rows
    chunk, head = my_place(heads)
    lane = lane_of((rows, LANES))
    spot = (row_order(rows, plan.rates, (rows, LANES), 0) + head) & (rows - 1)
    start, stop = doc_lanes(doc_ref, rows)
    low, high = lane_mask(rows, 1.0, 0.0), lane_mask(rows, 0.0, 1.0)
    low_scaled = lane_mask(rows, HEAD_DIM**-0.5, 0.0)
    for j in range(heads):
        token = (chunk * heads + j) * rows + spot
        marked = (token >= start) & (token < stop)
        qg, kv = x_ref[j, 0], x_ref[j, 1]
        qa[j] = qg * low_scaled + jnp.where(marked, 1.0, 0.0).astype(jnp.bfloat16)
        ka[j] = kv * low + key_lanes(marked, lane, None)
        va[j] = kv * high + low
        ga[j] = qg * high
    for level, (count, span) in enumerate(plan.near):
        for key_blocks, blocks in tiles(plan, count, span):
            peak, summed = forward(*(rows_of(r, b, count) for r, b in ((qa, blocks), (ka, key_blocks), (va, key_blocks))))
            if level > 0:
                peak, summed = merged(rows_of(top, blocks, count), rows_of(acc, blocks, count), peak, summed)
            set_rows(top, blocks, count, peak)
            set_rows(acc, blocks, count, summed)


def pieces(x):
    first = x.astype(jnp.bfloat16).astype(jnp.float32)
    second = (x - first).astype(jnp.bfloat16).astype(jnp.float32)
    return first, second, x - first - second


def far_kernel(plan, doc_ref, qa, ka, va, ga, acc_in, top_in, *refs):
    levels = len(plan.far)
    far_in, refs = refs[:levels], refs[levels:]
    (qb, gb, output), refs = refs[:3], refs[3:]
    far_dq, far_dkv, far_out, (acc, top) = refs[:levels], refs[levels : 2 * levels], refs[2 * levels : -2], refs[-2:]
    heads, rows = plan.heads, plan.rows
    every = range(heads)
    _, reach = plan.late
    for j in every:
        acc[j], top[j] = acc_in[j, 0:reach], top_in[j, 0:reach]
    for level, (_, held, _) in enumerate(plan.far):
        peak, summed = forward(*far_operands(plan, level, doc_ref, qa, ka, va, far_in[level]))
        peak, summed = merged(rows_of(top, every, held), rows_of(acc, every, held), peak, summed)
        set_rows(top, every, held, peak)
        set_rows(acc, every, held, summed)

    lane = lane_of((rows, LANES))
    total, peak, dots = jnp.ones((rows, LANES), jnp.float32), *[jnp.zeros((rows, LANES), jnp.float32)] * 2
    sums = []
    for j in every:
        sums.append(jnp.concatenate([acc[j], acc_in[j, reach:]], axis=0))
        dot_j = jnp.sum(sums[j] * ga[j].astype(jnp.float32), axis=1, keepdims=True)
        total = jnp.where(lane == j, sums[j], total)
        peak = jnp.where(lane == j, jnp.concatenate([top[j], top_in[j, reach:]], axis=0), peak)
        dots = jnp.where(lane == j, dot_j, dots)
    inverse = 1.0 / total
    held_pieces = [*pieces(-(peak + jnp.log(total))), *pieces(-(dots * inverse))]
    moved = held_pieces[0]
    for i, piece in enumerate(held_pieces[1:]):
        moved = moved + pltpu.roll(piece, (i + 1) * heads, 1)
    moved = moved.astype(jnp.bfloat16)
    column = lane_of((LANES, 2 * LANES))
    source = lax.broadcasted_iota(jnp.int32, column.shape, 0)
    wanted = jnp.full(column.shape, -LANES, jnp.int32)
    for i in range(3):
        wanted = jnp.where(column == TOTAL_LANE + i, i * heads, wanted)
        wanted = jnp.where(column == LANES + i, (3 + i) * heads, wanted)
    wanted = source - wanted
    for j in every:
        place_j = jnp.where(wanted == j, 1.0, 0.0).astype(jnp.bfloat16)
        added = dot(moved, place_j, (1, 0)).astype(jnp.bfloat16)
        qb[j] = qa[j] + added[:, :LANES]
        gb[j] = ga[j] + added[:, LANES:]
        output[j] = sums[j] * inverse[:, j : j + 1]

    for level, (_, held, chunks) in enumerate(plan.far):
        queries, keys, values = far_operands(plan, level, doc_ref, qb, ka, va, far_in[level])
        for_queries, for_keys = backward(queries, rows_of(gb, every, held), keys, values)
        size = heads * held
        far_dq[level][...] = for_queries
        far_dkv[level][...] = for_keys[:size]
        for i in range(1, chunks):
            far_out[level][i - 1] = for_keys[i * size : (i + 1) * size].astype(jnp.bfloat16)


def local_kernel(plan, qb, ka, va, gb, dq, dkv):
    for level, (count, span) in enumerate(plan.near[:2]):
        for key_blocks, blocks in tiles(plan, count, span):
            for_queries, for_keys = backward(
                *(rows_of(r, b, count) for r, b in ((qb, blocks), (gb, blocks), (ka, key_blocks), (va, key_blocks)))
            )
            (add_rows if level else set_rows)(dq, blocks, count, for_queries)
            fresh = level == 0 and blocks.start == key_blocks.start
            (set_rows if fresh else add_rows)(dkv, key_blocks, count, for_keys)


def last_kernel(plan, qb, ka, va, gb, output, dq_in, dkv_in, *refs):
    levels = len(plan.far)
    far_dq, far_dkv, far_back = refs[:levels], refs[levels : 2 * levels], refs[2 * levels : 3 * levels]
    out_ref, dq, dkv = refs[3 * levels :]
    heads, rows = plan.heads, plan.rows
    every, (near, reach) = range(heads), plan.late
    for j in every:
        dq[j], dkv[j] = dq_in[j, 0:reach], dkv_in[j, 0:reach]
    for count, span in near:
        for key_blocks, blocks in tiles(plan, count, span):
            for_queries, for_keys = backward(
                *(rows_of(r, b, count) for r, b in ((qb, blocks), (gb, blocks), (ka, key_blocks), (va, key_blocks)))
            )
            add_rows(dq, blocks, count, for_queries)
            add_rows(dkv, key_blocks, count, for_keys)
    for level, (_, held, chunks) in enumerate(plan.far):
        add_rows(dq, every, held, far_dq[level][...])
        partial = far_dkv[level][...]
        for i in range(1, chunks):
            partial = partial + far_back[level][i - 1].astype(jnp.float32)
        add_rows(dkv, every, held, partial)
    low = lane_of((rows, LANES)) < HEAD_DIM
    for j in every:
        for_queries = jnp.concatenate([dq[j], dq_in[j, reach:]], axis=0)
        out_ref[j, 0] = jnp.where(low, for_queries * HEAD_DIM**-0.5, output[j]).astype(jnp.bfloat16)
        out_ref[j, 1] = jnp.concatenate([dkv[j], dkv_in[j, reach:]], axis=0).astype(jnp.bfloat16)


def landed(x):
    return pltpu.VMEM(x.shape, x.dtype)


def call(kernel, out_shapes, args, scratch=(), flops=0, inputs=pltpu.VMEM, outputs=pltpu.VMEM, limit=VMEM_LIMIT):
    moved = sum(x.size * x.dtype.itemsize for x in (*args, *out_shapes))
    return pl.pallas_call(
        kernel,
        out_shape=out_shapes,
        in_specs=[pl.BlockSpec(memory_space=inputs)] * len(args),
        out_specs=[pl.BlockSpec(memory_space=outputs)] * len(out_shapes),
        scratch_shapes=scratch,
        compiler_params=pltpu.CompilerParams(vmem_limit_bytes=limit),
        cost_estimate=pl.CostEstimate(flops=flops, bytes_accessed=moved, transcendentals=0),
    )(*args)


def body(queries, keys, values, grad_out, doc_ids):
    rows, width = queries.shape
    shards, parts = lax.axis_size("seq"), lax.axis_size("head")
    devices, axes = shards * parts, ("seq", "head")
    plan = plan_of(rows, width, shards, parts)
    heads, _, (_, reach) = plan.heads, plan.far, plan.late
    groups = [[c * heads + h for h in range(heads)] for c in range(devices // heads)]

    def exchange(x):
        return lax.all_to_all(x, axes, 0, 0, axis_index_groups=groups, tiled=True)

    def from_chunk(x, i):
        return lax.ppermute(x, axes, [(d, d ^ (i * heads)) for d in range(devices)])

    def run(kernel, *rest, **more):
        return call(functools.partial(kernel, plan), *rest, **more)

    shape, low, full = jax.ShapeDtypeStruct, jnp.bfloat16, jnp.float32
    packed = shape((heads, 2, rows, LANES), low)
    operand, total = shape((heads, rows, LANES), low), shape((heads, rows, LANES), full)
    prefix = shape((heads, reach, LANES), full)
    own_far = [shape((heads * held, LANES), full) for _, held, _ in plan.far]
    docs = doc_ids.reshape(-1, LANES)

    inputs = (queries, keys, values, grad_out)
    semaphores = pltpu.SemaphoreType.DMA((COPY_PARTS, len(inputs)))
    landing = [landed(x) for x in (*inputs, packed)]
    landing += [pltpu.SemaphoreType.DMA((len(inputs),)), pltpu.SemaphoreType.DMA((2, COPY_PARTS))]
    mine = call(
        functools.partial(pack_kernel, plan.rates), [packed], inputs, landing, flops=1 << 27, inputs=pltpu.HBM, outputs=pltpu.HBM, limit=PACK_LIMIT
    )[0]
    chunk = exchange(mine)
    gathered = []
    for _, held, chunks in plan.far:
        picked = chunk[:, 1, :held].reshape(heads * held, LANES)
        gathered.append(jnp.stack([from_chunk(picked, i) for i in range(1, chunks)]))
    qa, ka, va, ga, acc, top = run(near_kernel, [operand] * 4 + [total] * 2, (docs, chunk), flops=1 << 30)
    sent = [shape(x.shape, x.dtype) for x in gathered]
    qb, gb, output, *rest = run(
        far_kernel,
        [operand] * 2 + [total] + own_far * 2 + sent,
        (docs, qa, ka, va, ga, acc, top, *gathered),
        [landed(prefix)] * 2,
        flops=1 << 28,
    )
    owned, partials = rest[: 2 * len(plan.far)], rest[2 * len(plan.far) :]
    returned = [jnp.stack([from_chunk(x[i], i + 1) for i in range(x.shape[0])]) for x in partials]
    dq, dkv = run(local_kernel, [total] * 2, (qb, ka, va, gb), flops=1 << 30)
    grads = run(
        last_kernel, [packed], (qb, ka, va, gb, output, dq, dkv, *owned, *returned), [landed(prefix)] * 2, flops=1 << 28
    )[0]
    result = [shape((rows, width), low)] * 4
    leaving = [landed(x) for x in result] + [semaphores]
    unpack = functools.partial(unpack_kernel, plan.rates)
    return tuple(call(unpack, result, (exchange(grads),), leaving, flops=1 << 27, outputs=pltpu.HBM))


def solution(mesh):
    split = P(("seq", "head"), None)
    return jax.shard_map(
        body, mesh=mesh, in_specs=(split,) * 4 + (P(),), out_specs=(split,) * 4, check_vma=False
    )
```

```python
import dataclasses
import functools

import jax
import jax.numpy as jnp
from jax import lax
from jax.experimental import pallas as pl
from jax.experimental.pallas import tpu as pltpu
from jax.sharding import PartitionSpec as P

HEAD_DIM = 64
LANES = 2 * HEAD_DIM
HIDDEN = -131072.0
DOC_LANE, TOTAL_LANE, QUERY_PAD, KEY_PAD = HEAD_DIM, HEAD_DIM + 3, HEAD_DIM + 6, HEAD_DIM + 7
QUERY_TILE = 256
FAR_ROWS = 8
COPY_PARTS = 2
PACK_LIMIT = 56 * 1024 * 1024
VMEM_LIMIT = 14 * 1024 * 1024


def dot(a, b, contract):
    return lax.dot_general(a, b, ((contract[:1], contract[1:]), ((), ())), preferred_element_type=jnp.float32)


def row_order(rows, rates, shape, axis):
    row = lax.broadcasted_iota(jnp.int32, shape, axis)
    order = row * rates[-1]
    for rate, above in zip(rates[-2::-1], rates[:0:-1]):
        between, fresh = above // rate - 1, row - rows // above
        if between > 0:
            group = fresh if between == 1 else lax.div(fresh, between)
            order = jnp.where(fresh >= 0, group * above + (fresh - group * between + 1) * rate, order)
    return order


def lane_of(shape):
    return lax.broadcasted_iota(jnp.int32, shape, 1)


def halves_swapped(x):
    return jnp.concatenate([x[:, HEAD_DIM:], x[:, :HEAD_DIM]], axis=1)


def lane_mask(rows, at_low, at_high):
    return jnp.where(lane_of((rows, LANES)) < HEAD_DIM, at_low, at_high).astype(jnp.bfloat16)


def pack_kernel(rates, q_hbm, k_hbm, v_hbm, g_hbm, out_hbm, q_ref, k_ref, v_ref, g_ref, out_ref, arrived, left):
    rows, width = q_ref.shape
    heads = width // HEAD_DIM
    held = ((k_hbm, k_ref), (v_hbm, v_ref), (q_hbm, q_ref), (g_hbm, g_ref))
    copies = [pltpu.make_async_copy(a, b, arrived.at[i]) for i, (a, b) in enumerate(held)]
    for copy in copies:
        copy.start()
    order = row_order(rows, rates, (rows, rows), 0)
    lane = lane_of((rows, rows))
    low, high = lane_mask(rows, 1.0, 0.0), lane_mask(rows, 0.0, 1.0)
    outgoing = []
    for kind, first_ref, second_ref, waits in ((1, k_ref, v_ref, copies[:2]), (0, q_ref, g_ref, copies[2:])):
        for copy in waits:
            copy.wait()
        for tile in range(width // LANES):
            cols = slice(tile * LANES, (tile + 1) * LANES)
            first, second = first_ref[:, cols], second_ref[:, cols]
            even = first * low + halves_swapped(second) * high
            odd = halves_swapped(first) * low + second * high
            for side, source in enumerate((even, odd)):
                pick = jnp.where(order == ((lane - (2 * tile + side)) & (rows - 1)), 1.0, 0.0).astype(jnp.bfloat16)
                out_ref[2 * tile + side, kind] = dot(pick, source, (1, 0)).astype(jnp.bfloat16)
            if (2 * tile + 2) % (heads // COPY_PARTS) == 0:
                done = pl.ds(2 * tile + 2 - heads // COPY_PARTS, heads // COPY_PARTS)
                ready = left.at[kind, (2 * tile + 1) // (heads // COPY_PARTS)]
                outgoing.append(pltpu.make_async_copy(out_ref.at[done, kind], out_hbm.at[done, kind], ready))
                outgoing[-1].start()
    for copy in outgoing:
        copy.wait()


def unpack_kernel(rates, in_ref, *refs):
    (out_hbm, dq_hbm, dk_hbm, dv_hbm), (out_ref, dq_ref, dk_ref, dv_ref, left) = refs[:4], refs[4:]
    rows, width = out_ref.shape
    outgoing = []
    order = row_order(rows, rates, (rows, rows), 1)
    token = lax.broadcasted_iota(jnp.int32, (rows, rows), 0)
    low, high = lane_mask(rows, 1.0, 0.0), lane_mask(rows, 0.0, 1.0)
    held = ((dq_ref, dq_hbm), (out_ref, out_hbm), (dk_ref, dk_hbm), (dv_ref, dv_hbm))
    for kind in range(2):
        for tile in range(width // LANES):
            cols = slice(tile * LANES, (tile + 1) * LANES)
            picks, sources = [], []
            for side in range(2):
                head = 2 * tile + side
                picks.append(jnp.where(((order + head) & (rows - 1)) == token, 1.0, 0.0).astype(jnp.bfloat16))
                x = in_ref[head, kind]
                y = halves_swapped(x)
                sources.append(jnp.concatenate([y * high, x * high] if side else [x * low, y * low], axis=1))
            moved = dot(jnp.concatenate(picks, axis=1), jnp.concatenate(sources, axis=0), (1, 0)).astype(jnp.bfloat16)
            for i in range(2):
                held[2 * kind + i][0][:, cols] = moved[:, i * LANES : (i + 1) * LANES]
        for i in range(2 * kind, 2 * kind + 2):
            outgoing.append(pltpu.make_async_copy(*held[i], left.at[0, i]))
            outgoing[-1].start()
    for copy in outgoing:
        copy.wait()


@dataclasses.dataclass(frozen=True)
class Plan:
    heads: int
    rows: int
    rates: tuple
    near: tuple
    far: tuple

    @property
    def late(self):
        return self.near[2:], max([count for count, _ in self.near[2:]] + [held for _, held, _ in self.far])


def plan_of(rows, width, shards, parts):
    heads, rates = width // HEAD_DIM, (1, 2, 8, shards)
    near, far = [], []
    for rate in rates:
        span = rows * parts * rate
        if span <= rows * heads:
            near.append((rows // rate, span // rows))
        else:
            far.append((rows // rate, max(rows // rate, FAR_ROWS), span // (rows * heads)))
    return Plan(heads, rows, rates, tuple(near), tuple(far))


def my_place(heads):
    index = lax.axis_index("seq") * lax.axis_size("head") + lax.axis_index("head")
    return lax.div(index, heads), index & (heads - 1)


def rows_of(ref, blocks, count):
    if count == ref.shape[1]:
        return ref[blocks.start : blocks.stop].reshape(len(blocks) * count, LANES)
    if ref.dtype == jnp.bfloat16 and count % 16:
        held = -(-count // 16) * 16
        parts = [ref[j, 0:held].astype(jnp.float32)[0:count] for j in blocks]
        return jnp.concatenate(parts, axis=0).astype(jnp.bfloat16)
    return jnp.concatenate([ref[j, 0:count] for j in blocks], axis=0)


def set_rows(ref, blocks, count, value):
    for i, j in enumerate(blocks):
        ref[j, 0:count] = value[i * count : (i + 1) * count]


def add_rows(ref, blocks, count, value):
    set_rows(ref, blocks, count, rows_of(ref, blocks, count) + value)


def doc_lanes(doc_ref, rows):
    docs = doc_ref[...]
    first, second = [jnp.sum(jnp.where(docs < d, 1, 0)) for d in (1, 2)]
    lane, last = lane_of((rows, LANES)), jnp.iinfo(jnp.int32).max
    start, stop = jnp.full((rows, LANES), last, jnp.int32), jnp.full((rows, LANES), 0, jnp.int32)
    for at, lo, hi in ((0, 0, first), (1, first, second), (2, second, last), (KEY_PAD - DOC_LANE, 0, last)):
        start = jnp.where(lane == DOC_LANE + at, lo, start)
        stop = jnp.where(lane == DOC_LANE + at, hi, stop)
    return start, stop


def key_lanes(marked, lane, padding):
    outside = jnp.where((lane >= TOTAL_LANE) & (lane <= QUERY_PAD), 1.0, 0.0)
    outside = jnp.where((lane >= DOC_LANE) & (lane < TOTAL_LANE), HIDDEN, outside)
    value = jnp.where(marked, 0.0, outside)
    if padding is not None:
        value = jnp.where((lane == KEY_PAD) & padding, HIDDEN, value)
    return value.astype(jnp.bfloat16)


def far_operands(plan, level, doc_ref, qa, ka, va, far_ref):
    count, held, chunks = plan.far[level]
    heads, rows = plan.heads, plan.rows
    chunk, head = my_place(heads)
    every, shape = range(heads), (heads * held, LANES)
    lane, index = lane_of(shape), lax.broadcasted_iota(jnp.int32, shape, 0)
    low, high = lane_mask(shape[0], 1.0, 0.0), lane_mask(shape[0], 0.0, 1.0)
    padding = None if count == held else (index & (held - 1)) >= count
    queries = rows_of(qa, every, held)
    key_sets, value_sets = [rows_of(ka, every, held)], [rows_of(va, every, held)]
    if padding is not None:
        queries = jnp.where((lane == QUERY_PAD) & padding, HIDDEN, queries.astype(jnp.float32)).astype(jnp.bfloat16)
        own = jnp.where((lane == KEY_PAD) & padding, HIDDEN, key_sets[0].astype(jnp.float32))
        key_sets[0] = own.astype(jnp.bfloat16)
    start, stop = doc_lanes(doc_ref, shape[0])
    order = row_order(rows, plan.rates, (held, LANES), 0)
    spots = jnp.concatenate([(order + head) & (rows - 1)] * heads, axis=0)
    for i in range(1, chunks):
        token = ((chunk ^ i) * heads + lax.div(index, held)) * rows + spots
        marked = (token >= start) & (token < stop)
        key_sets.append(far_ref[i - 1] * low + key_lanes(marked, lane, padding))
        value_sets.append(far_ref[i - 1] * high + low)
    return queries, jnp.concatenate(key_sets, axis=0), jnp.concatenate(value_sets, axis=0)


def forward(queries, keys, values):
    scores = dot(queries, keys, (1, 1))
    peak = jnp.max(scores, axis=1, keepdims=True)
    weights = jnp.exp(scores - peak).astype(jnp.bfloat16)
    return jnp.broadcast_to(peak, (queries.shape[0], LANES)), dot(weights, values, (1, 0))


def backward(queries, upstream, keys, values):
    probability = jnp.exp(dot(keys, queries, (1, 1)))
    shifted = (probability * dot(values, upstream, (1, 1))).astype(jnp.bfloat16)
    for_keys = dot(shifted, queries, (1, 0))
    for_values = dot(probability.astype(jnp.bfloat16), upstream, (1, 0))
    key_low = lane_of(for_keys.shape) < HEAD_DIM
    for_queries = dot(keys.T[:HEAD_DIM], shifted, (1, 0)).T
    for_queries = jnp.concatenate([for_queries, jnp.zeros_like(for_queries)], axis=1)
    return for_queries, jnp.where(key_low, for_keys, for_values)


def merged(old_peak, old, peak, summed):
    new_peak = jnp.maximum(old_peak, peak)
    return new_peak, old * jnp.exp(old_peak - new_peak) + summed * jnp.exp(peak - new_peak)


def tiles(plan, count, span):
    per_tile = max(1, QUERY_TILE // count)
    for start in range(0, plan.heads, span):
        for begin in range(start, start + span, per_tile):
            yield range(start, start + span), range(begin, min(begin + per_tile, start + span))


def near_kernel(plan, doc_ref, x_ref, qa, ka, va, ga, acc, top):
    heads, rows = plan.heads, plan.rows
    chunk, head = my_place(heads)
    lane = lane_of((rows, LANES))
    spot = (row_order(rows, plan.rates, (rows, LANES), 0) + head) & (rows - 1)
    start, stop = doc_lanes(doc_ref, rows)
    low, high = lane_mask(rows, 1.0, 0.0), lane_mask(rows, 0.0, 1.0)
    low_scaled = lane_mask(rows, HEAD_DIM**-0.5, 0.0)
    for j in range(heads):
        token = (chunk * heads + j) * rows + spot
        marked = (token >= start) & (token < stop)
        qg, kv = x_ref[j, 0], x_ref[j, 1]
        qa[j] = qg * low_scaled + jnp.where(marked, 1.0, 0.0).astype(jnp.bfloat16)
        ka[j] = kv * low + key_lanes(marked, lane, None)
        va[j] = kv * high + low
        ga[j] = qg * high
    for level, (count, span) in enumerate(plan.near):
        for key_blocks, blocks in tiles(plan, count, span):
            peak, summed = forward(*(rows_of(r, b, count) for r, b in ((qa, blocks), (ka, key_blocks), (va, key_blocks))))
            if level > 0:
                peak, summed = merged(rows_of(top, blocks, count), rows_of(acc, blocks, count), peak, summed)
            set_rows(top, blocks, count, peak)
            set_rows(acc, blocks, count, summed)


def pieces(x):
    first = x.astype(jnp.bfloat16).astype(jnp.float32)
    second = (x - first).astype(jnp.bfloat16).astype(jnp.float32)
    return first, second, x - first - second


def far_kernel(plan, doc_ref, qa, ka, va, ga, acc_in, top_in, *refs):
    levels = len(plan.far)
    far_in, refs = refs[:levels], refs[levels:]
    (qb, gb, output), refs = refs[:3], refs[3:]
    far_dq, far_dkv, far_out, (acc, top) = refs[:levels], refs[levels : 2 * levels], refs[2 * levels : -2], refs[-2:]
    heads, rows = plan.heads, plan.rows
    every = range(heads)
    _, reach = plan.late
    for j in every:
        acc[j], top[j] = acc_in[j, 0:reach], top_in[j, 0:reach]
    for level, (_, held, _) in enumerate(plan.far):
        peak, summed = forward(*far_operands(plan, level, doc_ref, qa, ka, va, far_in[level]))
        peak, summed = merged(rows_of(top, every, held), rows_of(acc, every, held), peak, summed)
        set_rows(top, every, held, peak)
        set_rows(acc, every, held, summed)

    lane = lane_of((rows, LANES))
    total, peak, dots = jnp.ones((rows, LANES), jnp.float32), *[jnp.zeros((rows, LANES), jnp.float32)] * 2
    sums = []
    for j in every:
        sums.append(jnp.concatenate([acc[j], acc_in[j, reach:]], axis=0))
        dot_j = jnp.sum(sums[j] * ga[j].astype(jnp.float32), axis=1, keepdims=True)
        total = jnp.where(lane == j, sums[j], total)
        peak = jnp.where(lane == j, jnp.concatenate([top[j], top_in[j, reach:]], axis=0), peak)
        dots = jnp.where(lane == j, dot_j, dots)
    inverse = 1.0 / total
    held_pieces = [*pieces(-(peak + jnp.log(total))), *pieces(-(dots * inverse))]
    moved = held_pieces[0]
    for i, piece in enumerate(held_pieces[1:]):
        moved = moved + pltpu.roll(piece, (i + 1) * heads, 1)
    moved = moved.astype(jnp.bfloat16)
    column = lane_of((LANES, 2 * LANES))
    source = lax.broadcasted_iota(jnp.int32, column.shape, 0)
    wanted = jnp.full(column.shape, -LANES, jnp.int32)
    for i in range(3):
        wanted = jnp.where(column == TOTAL_LANE + i, i * heads, wanted)
        wanted = jnp.where(column == LANES + i, (3 + i) * heads, wanted)
    wanted = source - wanted
    for j in every:
        place_j = jnp.where(wanted == j, 1.0, 0.0).astype(jnp.bfloat16)
        added = dot(moved, place_j, (1, 0)).astype(jnp.bfloat16)
        qb[j] = qa[j] + added[:, :LANES]
        gb[j] = ga[j] + added[:, LANES:]
        output[j] = sums[j] * inverse[:, j : j + 1]

    for level, (_, held, chunks) in enumerate(plan.far):
        queries, keys, values = far_operands(plan, level, doc_ref, qb, ka, va, far_in[level])
        for_queries, for_keys = backward(queries, rows_of(gb, every, held), keys, values)
        size = heads * held
        far_dq[level][...] = for_queries
        far_dkv[level][...] = for_keys[:size]
        for i in range(1, chunks):
            far_out[level][i - 1] = for_keys[i * size : (i + 1) * size].astype(jnp.bfloat16)


def local_kernel(plan, qb, ka, va, gb, dq, dkv):
    for level, (count, span) in enumerate(plan.near[:2]):
        for key_blocks, blocks in tiles(plan, count, span):
            for_queries, for_keys = backward(
                *(rows_of(r, b, count) for r, b in ((qb, blocks), (gb, blocks), (ka, key_blocks), (va, key_blocks)))
            )
            (add_rows if level else set_rows)(dq, blocks, count, for_queries)
            fresh = level == 0 and blocks.start == key_blocks.start
            (set_rows if fresh else add_rows)(dkv, key_blocks, count, for_keys)


def last_kernel(plan, qb, ka, va, gb, output, dq_in, dkv_in, *refs):
    levels = len(plan.far)
    far_dq, far_dkv, far_back = refs[:levels], refs[levels : 2 * levels], refs[2 * levels : 3 * levels]
    out_ref, dq, dkv = refs[3 * levels :]
    heads, rows = plan.heads, plan.rows
    every, (near, reach) = range(heads), plan.late
    for j in every:
        dq[j], dkv[j] = dq_in[j, 0:reach], dkv_in[j, 0:reach]
    for count, span in near:
        for key_blocks, blocks in tiles(plan, count, span):
            for_queries, for_keys = backward(
                *(rows_of(r, b, count) for r, b in ((qb, blocks), (gb, blocks), (ka, key_blocks), (va, key_blocks)))
            )
            add_rows(dq, blocks, count, for_queries)
            add_rows(dkv, key_blocks, count, for_keys)
    for level, (_, held, chunks) in enumerate(plan.far):
        add_rows(dq, every, held, far_dq[level][...])
        partial = far_dkv[level][...]
        for i in range(1, chunks):
            partial = partial + far_back[level][i - 1].astype(jnp.float32)
        add_rows(dkv, every, held, partial)
    low = lane_of((rows, LANES)) < HEAD_DIM
    for j in every:
        for_queries = jnp.concatenate([dq[j], dq_in[j, reach:]], axis=0)
        out_ref[j, 0] = jnp.where(low, for_queries * HEAD_DIM**-0.5, output[j]).astype(jnp.bfloat16)
        out_ref[j, 1] = jnp.concatenate([dkv[j], dkv_in[j, reach:]], axis=0).astype(jnp.bfloat16)


def landed(x):
    return pltpu.VMEM(x.shape, x.dtype)


def call(kernel, out_shapes, args, scratch=(), flops=0, inputs=pltpu.VMEM, outputs=pltpu.VMEM, limit=VMEM_LIMIT):
    moved = sum(x.size * x.dtype.itemsize for x in (*args, *out_shapes))
    return pl.pallas_call(
        kernel,
        out_shape=out_shapes,
        in_specs=[pl.BlockSpec(memory_space=inputs)] * len(args),
        out_specs=[pl.BlockSpec(memory_space=outputs)] * len(out_shapes),
        scratch_shapes=scratch,
        compiler_params=pltpu.CompilerParams(vmem_limit_bytes=limit),
        cost_estimate=pl.CostEstimate(flops=flops, bytes_accessed=moved, transcendentals=0),
    )(*args)


def body(queries, keys, values, grad_out, doc_ids):
    rows, width = queries.shape
    shards, parts = lax.axis_size("seq"), lax.axis_size("head")
    devices, axes = shards * parts, ("seq", "head")
    plan = plan_of(rows, width, shards, parts)
    heads, _, (_, reach) = plan.heads, plan.far, plan.late
    groups = [[c * heads + h for h in range(heads)] for c in range(devices // heads)]

    def exchange(x):
        return lax.all_to_all(x, axes, 0, 0, axis_index_groups=groups, tiled=True)

    def from_chunk(x, i):
        return lax.ppermute(x, axes, [(d, d ^ (i * heads)) for d in range(devices)])

    def run(kernel, *rest, **more):
        return call(functools.partial(kernel, plan), *rest, **more)

    shape, low, full = jax.ShapeDtypeStruct, jnp.bfloat16, jnp.float32
    packed = shape((heads, 2, rows, LANES), low)
    operand, total = shape((heads, rows, LANES), low), shape((heads, rows, LANES), full)
    prefix = shape((heads, reach, LANES), full)
    own_far = [shape((heads * held, LANES), full) for _, held, _ in plan.far]
    docs = doc_ids.reshape(-1, LANES)

    inputs = (queries, keys, values, grad_out)
    semaphores = pltpu.SemaphoreType.DMA((COPY_PARTS, len(inputs)))
    landing = [landed(x) for x in (*inputs, packed)]
    landing += [pltpu.SemaphoreType.DMA((len(inputs),)), pltpu.SemaphoreType.DMA((2, COPY_PARTS))]
    mine = call(
        functools.partial(pack_kernel, plan.rates), [packed], inputs, landing, flops=1 << 27, inputs=pltpu.HBM, outputs=pltpu.HBM, limit=PACK_LIMIT
    )[0]
    chunk = exchange(mine)
    gathered = []
    for _, held, chunks in plan.far:
        picked = chunk[:, 1, :held].reshape(heads * held, LANES)
        gathered.append(jnp.stack([from_chunk(picked, i) for i in range(1, chunks)]))
    qa, ka, va, ga, acc, top = run(near_kernel, [operand] * 4 + [total] * 2, (docs, chunk), flops=1 << 30)
    sent = [shape(x.shape, x.dtype) for x in gathered]
    qb, gb, output, *rest = run(
        far_kernel,
        [operand] * 2 + [total] + own_far * 2 + sent,
        (docs, qa, ka, va, ga, acc, top, *gathered),
        [landed(prefix)] * 2,
        flops=1 << 28,
    )
    owned, partials = rest[: 2 * len(plan.far)], rest[2 * len(plan.far) :]
    returned = [jnp.stack([from_chunk(x[i], i + 1) for i in range(x.shape[0])]) for x in partials]
    dq, dkv = run(local_kernel, [total] * 2, (qb, ka, va, gb), flops=1 << 30)
    grads = run(
        last_kernel, [packed], (qb, ka, va, gb, output, dq, dkv, *owned, *returned), [landed(prefix)] * 2, flops=1 << 28
    )[0]
    result = [shape((rows, width), low)] * 4
    leaving = [landed(x) for x in result] + [semaphores]
    unpack = functools.partial(unpack_kernel, plan.rates)
    return tuple(call(unpack, result, (exchange(grads),), leaving, flops=1 << 27, outputs=pltpu.HBM))


def solution(mesh):
    split = P(("seq", "head"), None)
    return jax.shard_map(
        body, mesh=mesh, in_specs=(split,) * 4 + (P(),), out_specs=(split,) * 4, check_vma=False
    )
```
